32 devices in a mesh: tile: 16 (over z, y, x), lev: 2 (over core).
Axes of the slice: x: 2, y: 2, z: 4, core: 2. Of those that a mesh axis runs over, the one named last changes fastest.
Arguments:
- state: bfloat16 [4, 64, 32, 512], P('lev', 'tile'), may hold values from -6 to 6
- w_qkv: bfloat16 [512, 1536], replicated, may hold values from -0.25 to 0.25
- w_out: bfloat16 [512, 512], replicated, may hold values from -0.25 to 0.25
- cotangent: bfloat16 [4, 64, 32, 512], P('lev', 'tile'), may hold values from -6 to 6
- ocean: int32 [16], replicated, may hold values from 0 to 1
- depth: int32 [16], replicated, may hold values from 1 to 4
Outputs:
- output: bfloat16 [4, 64, 32, 512], P('lev', 'tile')
- d_state: bfloat16 [4, 64, 32, 512], P('lev', 'tile')
- d_w_qkv: float32 [512, 1536], P(('tile', 'lev'))
- d_w_out: float32 [512, 512], P(('tile', 'lev'))
The draws below stay inside these ranges and needn't reach their ends.
All inputs are finite; a program needn't handle non-finite values.
Results may differ from the reference program's by a relative error of at most 0.01.
Values may be sent and summed in bfloat16 or wider, within the bound.
No kernel may reach another device: no remote copies, remote signals or barrier semaphores. Data moves between devices by JAX's collectives and lax.ppermute only.
A program may use at most 128 MiB of HBM per device.

```python
import jax
import jax.numpy as jnp
from jax import lax

D = 512
HEADS = 8
COLS = 32
BROWS = 4
R_DEV = 4
ROWS = 64
LEVELS = 4


def edge_blocks():
    count = ROWS // BROWS
    reach = 2 * R_DEV // BROWS
    index = jnp.arange(count)
    return (index < reach) | (index >= count - reach)


def draw_ocean(key, part):
    count = ROWS // BROWS
    coins = jax.random.randint(jax.random.fold_in(key, 11), (count,), 0, 4)
    sea = (coins < 3).astype(jnp.int32)
    return jnp.where(edge_blocks(), jnp.int32(1), sea).astype(jnp.int32)


def draw_depth(key, part):
    count = ROWS // BROWS
    levels_drawn = jax.random.randint(jax.random.fold_in(key, 23), (count,), 1, LEVELS + 1)
    return jnp.where(edge_blocks(), jnp.int32(LEVELS), levels_drawn).astype(jnp.int32)


def levels(own_key, shape, split, smallest, top_value):
    def one(axis_at, parts):
        steps = jax.random.uniform(jax.random.fold_in(jax.random.fold_in(own_key, 6), axis_at), (parts,), jnp.float32, smallest / len(split), top_value / len(split))
        return jnp.repeat(jnp.exp(steps), shape[axis_at] // parts).reshape((-1,) + (1,) * (len(shape) - axis_at - 1))

    gain = one(*split[0])
    for cut in split[1:]:
        gain = gain * one(*cut)
    return gain


def bell_draw(stream_key, shape, deviation, limit, shards=(), dtype=jnp.bfloat16):
    array = deviation * jax.random.normal(stream_key, shape, jnp.float32)
    if shards:
        array = array * levels(stream_key, shape, shards, -0.22, 0.18)
    return jnp.clip(array, -limit, limit).astype(dtype)


def setup_inputs(seed: int = 0) -> dict:
    seeds = jax.random.split(jax.random.key(seed), 7)
    state = bell_draw(seeds[0], (LEVELS, ROWS, COLS, D), 1.0, 6.0, ((0, 2), (1, 16)))
    w_qkv = bell_draw(seeds[1], (D, 3 * D), D ** -0.5, 0.25)
    w_out = bell_draw(seeds[2], (D, D), D ** -0.5, 0.25)
    cotangent = bell_draw(seeds[3], (LEVELS, ROWS, COLS, D), 1.0, 6.0, ((0, 2), (1, 16)))
    ocean = draw_ocean(jax.random.fold_in(seeds[6], 71), 0)
    depth = draw_depth(jax.random.fold_in(seeds[6], 71), 0)
    return {"state": state, "w_qkv": w_qkv, "w_out": w_out, "cotangent": cotangent, "ocean": ocean, "depth": depth}


def lookup(table, index):
    hits = index[:, None] == jnp.arange(table.shape[0])[None, :]
    return jnp.sum(jnp.where(hits, table[None, :], 0), axis=1)


def reference(state, w_qkv, w_out, cotangent, ocean, depth):
    model = D
    heads = HEADS
    head = model // heads
    scale = head ** -0.5
    flat = state.reshape(-1, model)
    cot_flat = cotangent.reshape(-1, model)
    row_ids = jnp.arange(ROWS)
    sea = lookup(ocean, row_ids // BROWS)
    floor_n = lookup(depth, row_ids // BROWS)
    live = (sea[None, :] == 1) & (jnp.arange(LEVELS)[:, None] < floor_n[None, :])
    live_f = live.astype(jnp.float32)
    qkv = jnp.dot(flat, w_qkv, preferred_element_type=jnp.float32).astype(jnp.bfloat16)
    qkv = qkv.reshape(LEVELS, ROWS, COLS, 3 * model)
    queries = qkv[..., :model]
    keys = qkv[..., model:2 * model]
    values = qkv[..., 2 * model:]
    upstream = jnp.dot(cot_flat, w_out.T, preferred_element_type=jnp.float32).astype(jnp.bfloat16)
    upstream = upstream.reshape(LEVELS, ROWS, COLS, model) * live[:, :, None, None].astype(jnp.bfloat16)
    pad_spec = ((1, 1), (3, 3), (0, 0), (0, 0))
    keys_pad = jnp.pad(keys, pad_spec)
    values_pad = jnp.pad(values, pad_spec)
    live_pad = jnp.pad(live_f, ((1, 1), (3, 3)))
    cols = jnp.arange(COLS)
    near_cols = jnp.abs(cols[:, None] - cols[None, :]) <= 3
    grads_k = jnp.zeros((LEVELS + 2, ROWS + 6, COLS, model), jnp.float32)
    grads_v = jnp.zeros((LEVELS + 2, ROWS + 6, COLS, model), jnp.float32)
    attn_all = jnp.zeros((LEVELS, ROWS, COLS, model), jnp.bfloat16)
    dq_all = jnp.zeros((LEVELS, ROWS, COLS, model), jnp.bfloat16)

    def step(index, carry):
        grads_k, grads_v, attn_all, dq_all = carry
        lev = (index // ROWS).astype(jnp.int32)
        row = (index % ROWS).astype(jnp.int32)
        zero = jnp.int32(0)
        qrow = lax.dynamic_slice(queries, (lev, row, zero, zero), (1, 1, COLS, model)).reshape(COLS, heads, head).astype(jnp.float32)
        drow = lax.dynamic_slice(upstream, (lev, row, zero, zero), (1, 1, COLS, model)).reshape(COLS, heads, head).astype(jnp.float32)
        kwin = lax.dynamic_slice(keys_pad, (lev, row, zero, zero), (3, 7, COLS, model)).reshape(-1, heads, head).astype(jnp.float32)
        vwin = lax.dynamic_slice(values_pad, (lev, row, zero, zero), (3, 7, COLS, model)).reshape(-1, heads, head).astype(jnp.float32)
        lwin = lax.dynamic_slice(live_pad, (lev, row), (3, 7))
        qlive = lax.dynamic_slice(live_f, (lev, row), (1, 1))[0, 0]
        mask = near_cols[:, None, None, :] & (lwin[None, :, :, None] > 0)
        mask = jnp.broadcast_to(mask, (COLS, 3, 7, COLS)).reshape(COLS, -1)
        scores = jnp.einsum('qhe,khe->hqk', qrow, kwin) * scale
        scores = jnp.where(mask[None], scores, -1e30)
        top = jnp.max(scores, axis=-1, keepdims=True)
        expo = jnp.exp(scores - top)
        prob = expo / jnp.sum(expo, axis=-1, keepdims=True)
        prob16 = lax.optimization_barrier(prob.astype(jnp.bfloat16)).astype(jnp.float32)
        attn = jnp.einsum('hqk,khe->qhe', prob16, vwin) * qlive
        dprob = jnp.einsum('qhe,khe->hqk', drow, vwin)
        dscore = prob * (dprob - jnp.sum(prob * dprob, axis=-1, keepdims=True)) * scale
        ds16 = lax.optimization_barrier(dscore.astype(jnp.bfloat16)).astype(jnp.float32)
        dq = jnp.einsum('hqk,khe->qhe', ds16, kwin)
        dk = jnp.einsum('hqk,qhe->khe', ds16, qrow).reshape(3, 7, COLS, model)
        dv = jnp.einsum('hqk,qhe->khe', prob16, drow).reshape(3, 7, COLS, model)
        start = (lev, row, zero, zero)
        grads_k = lax.dynamic_update_slice(grads_k, lax.dynamic_slice(grads_k, start, (3, 7, COLS, model)) + dk, start)
        grads_v = lax.dynamic_update_slice(grads_v, lax.dynamic_slice(grads_v, start, (3, 7, COLS, model)) + dv, start)
        attn_all = lax.dynamic_update_slice(attn_all, attn.reshape(1, 1, COLS, model).astype(jnp.bfloat16), start)
        dq_all = lax.dynamic_update_slice(dq_all, dq.reshape(1, 1, COLS, model).astype(jnp.bfloat16), start)
        return grads_k, grads_v, attn_all, dq_all

    grads_k, grads_v, attn_all, dq_all = lax.fori_loop(0, LEVELS * ROWS, step, (grads_k, grads_v, attn_all, dq_all))
    dk_all = grads_k[1:-1, 3:-3].astype(jnp.bfloat16)
    dv_all = grads_v[1:-1, 3:-3].astype(jnp.bfloat16)
    dqkv = jnp.concatenate([dq_all, dk_all, dv_all], axis=-1).reshape(-1, 3 * model)
    attn_flat = attn_all.reshape(-1, model)
    output = (flat.astype(jnp.float32) + jnp.dot(attn_flat, w_out, preferred_element_type=jnp.float32)).astype(jnp.bfloat16)
    d_state = (cot_flat.astype(jnp.float32) + jnp.dot(dqkv, w_qkv.T, preferred_element_type=jnp.float32)).astype(jnp.bfloat16)
    d_w_qkv = jnp.dot(flat.T, dqkv, preferred_element_type=jnp.float32)
    d_w_out = jnp.dot(attn_flat.T, cot_flat, preferred_element_type=jnp.float32)
    shape = (LEVELS, ROWS, COLS, model)
    return output.reshape(shape), d_state.reshape(shape), d_w_qkv, d_w_out
```

```python
import jax
import jax.numpy as jnp
from jax import lax
from jax.experimental import pallas as pl
from jax.experimental.pallas import tpu as pltpu
from jax.sharding import PartitionSpec as P

HEADS = 8
BROWS = 4
REACH = 3
GROUP = 4
PAIR = 2
LOW = -1e30
F32 = jnp.float32
BF16 = jnp.bfloat16


def dot(a, b, ca, cb):
    return lax.dot_general(a, b, (((ca,), (cb,)), ((), ())), preferred_element_type=F32)


def swap_pairs(count, first):
    route = []
    for i in range(first, count - 1, 2):
        route += [(i, i + 1), (i + 1, i)]
    return route


def kernel(with_odd, tiles, levs, *refs):
    ocean, depth, state, rows_e, rows_o, near_e, far_e = refs[:7]
    refs = refs[7:]
    if with_odd:
        near_o, far_o = refs[:2]
        refs = refs[2:]
    w_qkv, w_out, cot = refs[:3]
    out, own, dext, dw = refs[3:7]
    ext, kv, qs, us, attn, dq, dkv, dkv16, bias, live = refs[7:]
    levels_n, height, width, model = state.shape
    tall = height + 2 * REACH
    span = PAIR + 2 * REACH
    keys_n = 3 * span * width
    block = PAIR * width
    head = model // HEADS
    lanes_n = GROUP * head
    tile = lax.axis_index("tile")
    lev = lax.axis_index("lev")
    tile_odd = lax.rem(tile, 2)
    lev_odd = lax.rem(lev, 2)

    total_rows = height * tiles
    total_levels = levels_n * levs
    for r in range(tall):
        row = tile * height - REACH + r
        block_at = lax.div(jnp.clip(row, 0, total_rows - 1), BROWS)
        good = (row >= 0) & (row < total_rows) & (ocean[block_at] == 1)
        deep = depth[block_at]
        for l in range(levels_n + 2):
            at = lev * levels_n - 1 + l
            ok = good & (at >= 0) & (at < total_levels) & (at < deep)
            live[l * tall + r] = ok.astype(jnp.int32)

    ext[1 : levels_n + 1, REACH : height + REACH] = state[...]
    at_e = jnp.where(tile_odd == 0, height + REACH, 0)
    at_o = jnp.where(tile_odd == 0, 0, height + REACH)
    ext[1 : levels_n + 1, pl.ds(at_e, REACH)] = rows_e[...]
    ext[1 : levels_n + 1, pl.ds(at_o, REACH)] = rows_o[...]
    slot_e = jnp.where(lev_odd == 0, levels_n + 1, 0)
    slot_o = jnp.where(lev_odd == 0, 0, levels_n + 1)
    ext[slot_e, REACH : height + REACH] = near_e[...]
    ext[slot_e, pl.ds(at_e, REACH)] = far_e[0]
    ext[slot_e, pl.ds(at_o, REACH)] = far_e[1]
    if with_odd:
        ext[slot_o, REACH : height + REACH] = near_o[...]
        ext[slot_o, pl.ds(at_e, REACH)] = far_o[0]
        ext[slot_o, pl.ds(at_o, REACH)] = far_o[1]
    else:
        ext[slot_o] = jnp.zeros((tall, width, model), BF16)

    @pl.loop(0, levels_n + 2)
    def _(l):
        cells = ext[l].reshape(tall * width, model)
        pairs = dot(cells, w_qkv[:, model:], 1, 0).astype(BF16)
        kv[l] = pairs.reshape(tall, width, 2 * model)
        dkv[l] = jnp.zeros((tall, width, 2 * model), F32)

    for l in range(levels_n):
        flat = state[l].reshape(height * width, model)
        q = dot(flat, w_qkv[:, :model], 1, 0).astype(BF16) * jnp.asarray(head**-0.5, BF16)
        qs[l] = q.reshape(height, width, model)
        u = dot(cot[l].reshape(height * width, model), w_out[...], 1, 1).astype(BF16)
        u = u.reshape(height, width, model)
        for r in range(height):
            alive = live[(l + 1) * tall + REACH + r].astype(F32).astype(BF16)
            us[l, r] = u[r] * alive

    lane_head = lax.broadcasted_iota(jnp.int32, (block, lanes_n), 1) // head
    query = lax.broadcasted_iota(jnp.int32, (width, GROUP * block), 1) % block
    query_row = query // width
    query_col = query % width
    key_col = lax.broadcasted_iota(jnp.int32, (width, GROUP * block), 0)
    near_col = jnp.abs(key_col - query_col) <= REACH

    def spread(x):
        return jnp.concatenate(
            [jnp.where(lane_head == h, x, jnp.zeros_like(x)) for h in range(GROUP)], axis=0
        )

    def gather(x):
        total = jnp.where(lane_head == 0, x[:block], 0.0)
        for h in range(1, GROUP):
            total = jnp.where(lane_head == h, x[h * block : (h + 1) * block], total)
        return total

    pairs_n = height // PAIR

    @pl.loop(0, levels_n * pairs_n)
    def _(combo):
        l = combo // pairs_n
        r0 = (combo % pairs_n) * PAIR
        for dl in range(3):
            for kr in range(span):
                alive = live[(l + dl) * tall + r0 + kr] == 1
                near = near_col & (jnp.abs(query_row + REACH - kr) <= REACH)
                at = (dl * span + kr) * width
                bias[at : at + width] = jnp.where(near & alive, 0.0, LOW)
        for g in range(HEADS // GROUP):
            lanes = slice(g * lanes_n, (g + 1) * lanes_n)
            lanes_v = slice(model + g * lanes_n, model + (g + 1) * lanes_n)
            q = spread(qs[l, pl.ds(r0, PAIR), :, lanes].reshape(block, lanes_n))
            u = spread(us[l, pl.ds(r0, PAIR), :, lanes].reshape(block, lanes_n))
            k = kv[pl.ds(l, 3), pl.ds(r0, span), :, lanes].reshape(keys_n, lanes_n)
            v = kv[pl.ds(l, 3), pl.ds(r0, span), :, lanes_v].reshape(keys_n, lanes_n)
            s = dot(k, q, 1, 1) + bias[...]
            e = jnp.exp(s - jnp.max(s, axis=0, keepdims=True))
            p = e * (1.0 / jnp.sum(e, axis=0, keepdims=True))
            p16 = p.astype(BF16)
            dp = dot(v, u, 1, 1)
            ds = p * (dp - jnp.sum(p * dp, axis=0, keepdims=True))
            ds16 = ds.astype(BF16)
            a = gather(dot(p16, v, 0, 0))
            for r in range(PAIR):
                alive = live[(l + 1) * tall + REACH + r0 + r].astype(F32)
                attn[l, r0 + r, :, lanes] = (a[r * width : (r + 1) * width] * alive).astype(BF16)
            b = gather(dot(ds16, k, 0, 0)) * (head**-0.5)
            dq[l, pl.ds(r0, PAIR), :, lanes] = b.astype(BF16).reshape(PAIR, width, lanes_n)
            dk = dot(ds16, q, 1, 0).reshape(3, span, width, lanes_n)
            dkv[pl.ds(l, 3), pl.ds(r0, span), :, lanes] += dk
            dv = dot(p16, u, 1, 0).reshape(3, span, width, lanes_n)
            dkv[pl.ds(l, 3), pl.ds(r0, span), :, lanes_v] += dv

    for l in range(levels_n):
        flat = state[l].reshape(height * width, model)
        o = flat.astype(F32) + dot(attn[l].reshape(height * width, model), w_out[...], 1, 0)
        out[l] = o.astype(BF16).reshape(height, width, model)
        c = cot[l].reshape(height * width, model).astype(F32)
        c = c + dot(dq[l].reshape(height * width, model), w_qkv[:, :model], 1, 1)
        own[l] = c.reshape(height, width, model)

    @pl.loop(0, levels_n + 2)
    def _(l):
        d = dkv[l].astype(BF16)
        dkv16[l] = d
        part = dot(d.reshape(tall * width, 2 * model), w_qkv[:, model:], 1, 1)
        part = part.reshape(tall, width, model)
        dext[l] = part.astype(BF16)

        @pl.when((l > 0) & (l <= levels_n))
        def _():
            own[l - 1] += part[REACH : REACH + height]

    cells = levels_n * height * width
    dw[:, :model] = dot(state[...].reshape(cells, model), dq[...].reshape(cells, model), 0, 0)
    dw[:, 3 * model :] = dot(attn[...].reshape(cells, model), cot[...].reshape(cells, model), 0, 0)
    wide = (levels_n + 2) * tall * width
    for j in range(2):
        cols = slice(j * model, (j + 1) * model)
        dw[:, model + j * model : 2 * model + j * model] = dot(
            ext[...].reshape(wide, model), dkv16[:, :, :, cols].reshape(wide, model), 0, 0
        )


def pick(x, index, dim):
    return lax.dynamic_index_in_dim(x, index, dim, keepdims=False)


def scatter_stage(x, axis, dim, stride):
    radix = x.shape[dim]
    if radix == 1:
        return lax.index_in_dim(x, 0, dim, keepdims=False)
    count = lax.axis_size(axis)
    digit = lax.rem(lax.div(lax.axis_index(axis), stride), radix)
    total = pick(x, digit, dim)
    parts = []
    for k in range(1, radix):
        piece = pick(x, jnp.bitwise_xor(digit, k), dim).astype(BF16)
        parts.append(lax.ppermute(piece, axis, [(i, i ^ (k * stride)) for i in range(count)]))
    for part in parts:
        total = total + part.astype(F32)
    return total


def digits(count):
    sizes = []
    while count > 1:
        radix = 4 if count % 4 == 0 else 2
        sizes.append(radix)
        count //= radix
    return sizes


def scatter_sum(x):
    tiles, levs = lax.axis_size("tile"), lax.axis_size("lev")
    rows, cols = x.shape
    low_t, low_l = digits(tiles), digits(levs)
    shape = low_t[::-1] + low_l[::-1] + [rows // (tiles * levs), cols]
    x = x.reshape(shape)
    stride = 1
    for i, radix in enumerate(low_l):
        x = scatter_stage(x, "lev", len(low_t) + len(low_l) - 1 - i, stride)
        stride *= radix
    stride = 1
    for i, radix in enumerate(low_t):
        x = scatter_stage(x, "tile", len(low_t) - 1 - i, stride)
        stride *= radix
    return x


def local(state, w_qkv, w_out, cotangent, ocean, depth):
    levels_n, height, width, model = state.shape
    tiles, levs = lax.axis_size("tile"), lax.axis_size("lev")
    tile_odd = lax.rem(lax.axis_index("tile"), 2)
    lev_odd = lax.rem(lax.axis_index("lev"), 2)
    tall = height + 2 * REACH
    with_odd = levs > 2

    def swap(block, axis, first):
        return lax.ppermute(block, axis, swap_pairs(lax.axis_size(axis), first))

    top = height - REACH
    send_e = lax.dynamic_slice_in_dim(state, jnp.where(tile_odd == 0, top, 0), REACH, 1)
    send_o = lax.dynamic_slice_in_dim(state, jnp.where(tile_odd == 0, 0, top), REACH, 1)
    rows_e = swap(send_e, "tile", 0)
    rows_o = swap(send_o, "tile", 1)
    edge_e = jnp.where(lev_odd == 0, levels_n - 1, 0)
    edge_o = jnp.where(lev_odd == 0, 0, levels_n - 1)

    def far(edge):
        return jnp.stack([pick(rows_e, edge, 0), pick(rows_o, edge, 0)])

    levels = [swap(pick(state, edge_e, 0), "lev", 0), swap(far(edge_e), "lev", 0)]
    if with_odd:
        levels += [swap(pick(state, edge_o, 0), "lev", 1), swap(far(edge_o), "lev", 1)]

    smem = pl.BlockSpec(memory_space=pltpu.SMEM)
    vmem = pl.BlockSpec(memory_space=pltpu.VMEM)
    wide = (levels_n + 2, tall, width)
    own_cells = (levels_n, height, width, model)
    keys_n = 3 * (PAIR + 2 * REACH) * width
    out, own, dext, dw = pl.pallas_call(
        lambda *refs: kernel(with_odd, tiles, levs, *refs),
        out_shape=(
            jax.ShapeDtypeStruct(own_cells, BF16),
            jax.ShapeDtypeStruct(own_cells, F32),
            jax.ShapeDtypeStruct(wide + (model,), BF16),
            jax.ShapeDtypeStruct((model, 4 * model), F32),
        ),
        in_specs=[smem, smem] + [vmem] * (6 + len(levels)),
        out_specs=(vmem, vmem, vmem, vmem),
        scratch_shapes=[
            pltpu.VMEM(wide + (model,), BF16),
            pltpu.VMEM(wide + (2 * model,), BF16),
            pltpu.VMEM(own_cells, BF16),
            pltpu.VMEM(own_cells, BF16),
            pltpu.VMEM(own_cells, BF16),
            pltpu.VMEM(own_cells, BF16),
            pltpu.VMEM(wide + (2 * model,), F32),
            pltpu.VMEM(wide + (2 * model,), BF16),
            pltpu.VMEM((keys_n, GROUP * PAIR * width), F32),
            pltpu.SMEM(((levels_n + 2) * tall,), jnp.int32),
        ],
        compiler_params=pltpu.CompilerParams(vmem_limit_bytes=56 * 2**20),
    )(ocean, depth, state, rows_e, rows_o, *levels, w_qkv, w_out, cotangent)

    def onto(part, level):
        zero = jnp.zeros_like(part)
        return jnp.stack([jnp.where(level == l, part, zero) for l in range(levels_n)])

    slot_e = jnp.where(lev_odd == 0, levels_n + 1, 0)
    slot_o = jnp.where(lev_odd == 0, 0, levels_n + 1)
    across = onto(swap(pick(dext, slot_e, 0), "lev", 0).astype(F32), edge_e)
    if with_odd:
        across = across + onto(swap(pick(dext, slot_o, 0), "lev", 1).astype(F32), edge_o)
    at_e = jnp.where(tile_odd == 0, height + REACH, 0)
    at_o = jnp.where(tile_odd == 0, 0, height + REACH)

    def halo(at):
        mine = lax.dynamic_slice_in_dim(dext[1 : levels_n + 1], at, REACH, 1).astype(F32)
        return (mine + lax.dynamic_slice_in_dim(across, at, REACH, 1)).astype(BF16)

    back_e = swap(halo(at_e), "tile", 0).astype(F32)
    back_o = swap(halo(at_o), "tile", 1).astype(F32)
    above = jnp.where(tile_odd == 0, back_e, back_o)
    below = jnp.where(tile_odd == 0, back_o, back_e)
    rest = ((0, 0), (0, 0))
    d_state = own + across[:, REACH : REACH + height]
    d_state = d_state + jnp.pad(above, ((0, 0), (top, 0)) + rest)
    d_state = d_state + jnp.pad(below, ((0, 0), (0, top)) + rest)
    grads = scatter_sum(dw)
    return (out, d_state.astype(BF16), grads[:, : 3 * model], grads[:, 3 * model :])


def solution(mesh):
    placed = (P("lev", "tile", None, None), P(), P(), P("lev", "tile", None, None), P(), P())
    return jax.shard_map(
        local,
        mesh=mesh,
        in_specs=placed,
        out_specs=(
            P("lev", "tile", None, None),
            P("lev", "tile", None, None),
            P(("tile", "lev"), None),
            P(("tile", "lev"), None),
        ),
        check_vma=False,
    )
```

```python
import jax
import jax.numpy as jnp
from jax import lax
from jax.experimental import pallas as pl
from jax.experimental.pallas import tpu as pltpu
from jax.sharding import PartitionSpec as P

HEADS = 8
BROWS = 4
REACH = 3
GROUP = 4
PAIR = 2
LOW = -1e30
F32 = jnp.float32
BF16 = jnp.bfloat16
SMEM = pl.BlockSpec(memory_space=pltpu.SMEM)
VMEM = pl.BlockSpec(memory_space=pltpu.VMEM)


def dot(a, b, ca, cb):
    return lax.dot_general(a, b, (((ca,), (cb,)), ((), ())), preferred_element_type=F32)


def swap_pairs(count, first):
    route = []
    for i in range(first, count - 1, 2):
        route += [(i, i + 1), (i + 1, i)]
    return route


def call(body, name, outs, ins, scratch=(), mib=8, cost=10**6):
    return pl.pallas_call(
        body,
        name=name,
        out_shape=[jax.ShapeDtypeStruct(shape, kind) for shape, kind in outs],
        in_specs=[SMEM if x.dtype == jnp.int32 else VMEM for x in ins],
        out_specs=[VMEM] * len(outs),
        scratch_shapes=list(scratch),
        compiler_params=pltpu.CompilerParams(vmem_limit_bytes=mib * 2**20),
        cost_estimate=pl.CostEstimate(flops=cost, bytes_accessed=2**20, transcendentals=0),
    )(*ins)


class Plan:
    def __init__(self, shape, tiles, levs):
        self.levels_n, self.height, self.width, self.model = shape
        self.tiles, self.levs = tiles, levs
        self.tall = self.height + 2 * REACH
        self.compact = levs == 2 and self.levels_n == 2
        self.slots_n = self.levels_n + 2 - self.compact
        self.own = (self.levels_n, self.height, self.width)
        self.wide = (self.slots_n, self.tall, self.width)
        self.edge = (self.levels_n, REACH, self.width, self.model)

    def places(self):
        tile_odd = lax.rem(lax.axis_index("tile"), 2)
        lev_odd = lax.rem(lax.axis_index("lev"), 2)
        end = self.height + REACH
        self.even = tile_odd == 0
        self.at_e = jnp.where(tile_odd == 0, end, 0)
        self.at_o = jnp.where(tile_odd == 0, 0, end)
        self.off = 1 - lev_odd if self.compact else 0
        last = self.levels_n + 1
        self.slot_e = jnp.where(lev_odd == 0, last, 0) - self.off
        self.slot_o = jnp.where(lev_odd == 0, 0, last)
        self.first = 1 - self.off
        self.edge_e = jnp.where(lev_odd == 0, self.levels_n - 1, 0)
        self.edge_o = jnp.where(lev_odd == 0, 0, self.levels_n - 1)

    def liveness(self, ocean, depth, live):
        tile = lax.axis_index("tile")
        lev = lax.axis_index("lev")
        total_rows = self.height * self.tiles
        total_levels = self.levels_n * self.levs
        for r in range(self.tall):
            row = tile * self.height - REACH + r
            block_at = lax.div(jnp.clip(row, 0, total_rows - 1), BROWS)
            good = (row >= 0) & (row < total_rows) & (ocean[block_at] == 1)
            deep = depth[block_at]
            for l in range(self.levels_n + 2):
                at = lev * self.levels_n - 1 + l
                ok = good & (at >= 0) & (at < total_levels) & (at < deep)
                live[l * self.tall + r] = ok.astype(jnp.int32)

    def alive(self, live, level, row):
        return live[level * self.tall + row]


def stage_own(plan, ocean, depth, state, w_qkv, w_out, cot, *refs):
    near, (qs, us, mid, live) = refs[:-4], refs[-4:]
    height, width, model = plan.own[1:] + (plan.model,)
    cells = height * width
    head = model // HEADS
    plan.places()
    plan.liveness(ocean, depth, live)

    def pairs(x):
        y = dot(x.reshape(cells, model), w_qkv[:, model:], 1, 0).astype(BF16)
        return y.reshape(height, width, 2 * model)

    for l in range(plan.levels_n):
        mid[plan.first + l] = pairs(state[l])
        flat = state[l].reshape(cells, model)
        q = dot(flat, w_qkv[:, :model], 1, 0).astype(BF16) * jnp.asarray(head**-0.5, BF16)
        qs[l] = q.reshape(height, width, model)
        u = dot(cot[l].reshape(cells, model), w_out[...], 1, 1).astype(BF16)
        u = u.reshape(height, width, model)
        for r in range(height):
            us[l, r] = u[r] * plan.alive(live, l + 1, REACH + r).astype(F32).astype(BF16)
    mid[plan.slot_e] = pairs(near[0][plan.edge_o])
    if not plan.compact:
        mid[plan.slot_o] = pairs(near[1][plan.edge_e])


def stage_attend(plan, sums_n, ocean, depth, state, rows_e, rows_o, qs, us, mid, w_qkv, cot, *refs):
    sides = 1 if plan.compact else 2
    lev_in, refs = refs[: 3 * sides], refs[3 * sides :]
    attn, dq, dkv16 = refs[:3]
    sums, (ext, kv, dkv, bias, live) = refs[3 : 3 + sums_n], refs[3 + sums_n :]
    levels_n, height, width = plan.own
    model, tall = plan.model, plan.tall
    span = PAIR + 2 * REACH
    block = PAIR * width
    head = model // HEADS
    lanes_n = GROUP * head
    plan.places()
    plan.liveness(ocean, depth, live)

    inner = pl.ds(plan.first, levels_n)
    ext[inner, REACH : height + REACH] = state[...]
    ext[inner, pl.ds(plan.at_e, REACH)] = rows_e[...]
    ext[inner, pl.ds(plan.at_o, REACH)] = rows_o[...]
    for side, (slot, level) in enumerate(((plan.slot_e, plan.edge_o), (plan.slot_o, plan.edge_e))):
        if side < sides:
            near, far_e, far_o = lev_in[3 * side : 3 * side + 3]
            ext[slot, REACH : height + REACH] = near[level]
            ext[slot, pl.ds(plan.at_e, REACH)] = far_e[level]
            ext[slot, pl.ds(plan.at_o, REACH)] = far_o[level]

    @pl.loop(0, plan.slots_n)
    def _(l):
        edge = REACH * width
        cells = [ext[l, :REACH].reshape(edge, model), ext[l, height + REACH :].reshape(edge, model)]
        pairs = dot(jnp.concatenate(cells, axis=0), w_qkv[:, model:], 1, 0).astype(BF16)
        kv[l, :REACH] = pairs[:edge].reshape(REACH, width, 2 * model)
        kv[l, height + REACH :] = pairs[edge:].reshape(REACH, width, 2 * model)
        kv[l, REACH : height + REACH] = mid[l]
        dkv[l] = jnp.zeros((tall, width, 2 * model), F32)

    lane_head = lax.broadcasted_iota(jnp.int32, (block, lanes_n), 1) // head
    query = lax.broadcasted_iota(jnp.int32, (width, GROUP * block), 1) % block
    query_row = query // width
    query_col = query % width
    key_col = lax.broadcasted_iota(jnp.int32, (width, GROUP * block), 0)
    near_col = jnp.abs(key_col - query_col) <= REACH

    def spread(x):
        return jnp.concatenate(
            [jnp.where(lane_head == h, x, jnp.zeros_like(x)) for h in range(GROUP)], axis=0
        )

    def gather(x):
        total = jnp.where(lane_head == 0, x[:block], 0.0)
        for h in range(1, GROUP):
            total = jnp.where(lane_head == h, x[h * block : (h + 1) * block], total)
        return total

    def tile_step(l, r0, depth_n, base, base_level):
        keys_n = depth_n * span * width
        for dl in range(depth_n):
            for kr in range(span):
                alive = plan.alive(live, base_level + dl, r0 + kr) == 1
                near = near_col & (jnp.abs(query_row + REACH - kr) <= REACH)
                at = (dl * span + kr) * width
                bias[at : at + width] = jnp.where(near & alive, 0.0, LOW)
        for g in range(HEADS // GROUP):
            lanes = slice(g * lanes_n, (g + 1) * lanes_n)
            lanes_v = slice(model + g * lanes_n, model + (g + 1) * lanes_n)
            q = spread(qs[l, pl.ds(r0, PAIR), :, lanes].reshape(block, lanes_n))
            u = spread(us[l, pl.ds(r0, PAIR), :, lanes].reshape(block, lanes_n))
            k = kv[pl.ds(base, depth_n), pl.ds(r0, span), :, lanes].reshape(keys_n, lanes_n)
            v = kv[pl.ds(base, depth_n), pl.ds(r0, span), :, lanes_v].reshape(keys_n, lanes_n)
            s = dot(k, q, 1, 1) + bias[:keys_n]
            e = jnp.exp(s - jnp.max(s, axis=0, keepdims=True))
            p = e * (1.0 / jnp.sum(e, axis=0, keepdims=True))
            p16 = p.astype(BF16)
            dp = dot(v, u, 1, 1)
            ds = p * (dp - jnp.sum(p * dp, axis=0, keepdims=True))
            ds16 = ds.astype(BF16)
            a = gather(dot(p16, v, 0, 0))
            for r in range(PAIR):
                alive = plan.alive(live, l + 1, REACH + r0 + r).astype(F32)
                attn[l, r0 + r, :, lanes] = (a[r * width : (r + 1) * width] * alive).astype(BF16)
            b = gather(dot(ds16, k, 0, 0)) * (head**-0.5)
            dq[l, pl.ds(r0, PAIR), :, lanes] = b.astype(BF16).reshape(PAIR, width, lanes_n)
            dk = dot(ds16, q, 1, 0).reshape(depth_n, span, width, lanes_n)
            dkv[pl.ds(base, depth_n), pl.ds(r0, span), :, lanes] += dk
            dv = dot(p16, u, 1, 0).reshape(depth_n, span, width, lanes_n)
            dkv[pl.ds(base, depth_n), pl.ds(r0, span), :, lanes_v] += dv

    pairs_n = height // PAIR
    if plan.compact:

        @pl.loop(0, pairs_n)
        def _(pair):
            tile_step(plan.edge_e, pair * PAIR, 3, 0, plan.off)
            tile_step(plan.edge_o, pair * PAIR, 2, plan.first, 1)

    else:

        @pl.loop(0, levels_n * pairs_n)
        def _(combo):
            l = combo // pairs_n
            tile_step(l, (combo % pairs_n) * PAIR, 3, l, l)

    @pl.loop(0, plan.slots_n)
    def _(l):
        dkv16[l] = dkv[l].astype(BF16)

    cells = levels_n * height * width
    wide = plan.slots_n * tall * width

    def emit(at, x):
        n = x.shape[1]
        if sums_n == 1:
            sums[0][:, at : at + n] = x
            return
        keep, send = sums
        rows = model // (plan.tiles * plan.levs)
        x = x.reshape(plan.tiles, plan.levs, rows, n)
        mine = lax.axis_index("lev") == 0
        keep[:, :, at : at + n] = jnp.where(mine, x[:, 0], x[:, 1])
        send[:, :, at : at + n] = jnp.where(mine, x[:, 1], x[:, 0]).astype(BF16)

    emit(0, dot(state[...].reshape(cells, model), dq[...].reshape(cells, model), 0, 0))
    emit(3 * model, dot(attn[...].reshape(cells, model), cot[...].reshape(cells, model), 0, 0))
    for j in range(2):
        part = dkv16[:, :, :, j * model : (j + 1) * model].reshape(wide, model)
        emit((j + 1) * model, dot(ext[...].reshape(wide, model), part, 0, 0))


def stage_out(plan, state, cot, attn, dq, dkv16, w_qkv, w_out, out, own, rows_e, rows_o, *refs):
    edges, tmp = refs[:-1], refs[-1]
    levels_n, height, width = plan.own
    model, tall = plan.model, plan.tall
    cells = height * width
    plan.places()

    def back(slot):
        x = dot(dkv16[slot].reshape(tall * width, 2 * model), w_qkv[:, model:], 1, 1)
        return x.reshape(tall, width, model)

    for edge, slot in zip(edges, (plan.slot_e, plan.slot_o)):
        edge[...] = back(slot).astype(BF16)
    for l in range(levels_n):
        tmp[...] = back(plan.first + l)
        rows_e[l] = tmp[pl.ds(plan.at_e, REACH)]
        rows_o[l] = tmp[pl.ds(plan.at_o, REACH)]
        x = cot[l].reshape(cells, model).astype(F32)
        x = x + dot(dq[l].reshape(cells, model), w_qkv[:, :model], 1, 1)
        own[l] = x.reshape(height, width, model) + tmp[REACH : REACH + height]
        x = state[l].reshape(cells, model).astype(F32)
        x = x + dot(attn[l].reshape(cells, model), w_out[...], 1, 0)
        out[l] = x.astype(BF16).reshape(height, width, model)


def stage_fold(plan, rows_e, rows_o, *refs):
    edges, (send_e, send_o, acc) = refs[:-3], refs[-3:]
    plan.places()
    for rows, at, send in ((rows_e, plan.at_e, send_e), (rows_o, plan.at_o, send_o)):
        acc[...] = rows[...]
        for edge, level in zip(edges, (plan.edge_e, plan.edge_o)):
            acc[level] += edge[pl.ds(at, REACH)].astype(F32)
        send[...] = acc[...].astype(BF16)


def stage_last(plan, own, back_e, back_o, *refs):
    edges, (d_state, acc) = refs[:-2], refs[-2:]
    plan.places()
    height = plan.height
    acc[...] = own[...]
    for edge, level in zip(edges, (plan.edge_e, plan.edge_o)):
        acc[level] += edge[REACH : REACH + height].astype(F32)
    top = height - REACH
    acc[:, pl.ds(jnp.where(plan.even, top, 0), REACH)] += back_e[...].astype(F32)
    acc[:, pl.ds(jnp.where(plan.even, 0, top), REACH)] += back_o[...].astype(F32)
    d_state[...] = acc[...].astype(BF16)


def stage_split(parts_n, radix, stride, x, *refs):
    parts, (own, *pieces) = refs[:parts_n], refs[parts_n:]
    digit = lax.rem(lax.div(lax.axis_index("tile"), stride), radix)
    for h in range(x.shape[0] // radix):
        for k in range(radix):
            at = h * radix + jnp.bitwise_xor(digit, k)
            y = x[at]
            for part in parts:
                y = y + part[at].astype(F32)
            if k == 0:
                own[h] = y
            else:
                pieces[k - 1][h] = y.astype(BF16)


def stage_sum(parts_n, x, *refs):
    parts, (qkv, rest) = refs[:parts_n], refs[parts_n:]
    y = x[0]
    for part in parts:
        y = y + part[0].astype(F32)
    cut = qkv.shape[1]
    qkv[...] = y[:, :cut]
    rest[...] = y[:, cut:]


def digits(count):
    sizes = []
    while count > 1:
        radix = 4 if count % 4 == 0 else 2
        sizes.append(radix)
        count //= radix
    return sizes


def xor_route(count, step):
    return [(i, i ^ step) for i in range(count)]


def reduce_levels(x, tiles, levs):
    rows, cols = x.shape
    x = x.reshape([tiles] + digits(levs)[::-1] + [rows // (tiles * levs), cols])
    stride = 1
    for radix in digits(levs):
        dim = x.ndim - 3
        digit = lax.rem(lax.div(lax.axis_index("lev"), stride), radix)
        total = lax.dynamic_index_in_dim(x, digit, dim, keepdims=False)
        for k in range(1, radix):
            piece = lax.dynamic_index_in_dim(x, jnp.bitwise_xor(digit, k), dim, keepdims=False)
            piece = lax.ppermute(piece.astype(BF16), "lev", xor_route(levs, k * stride))
            total = total + piece.astype(F32)
        x = total
        stride *= radix
    return x


def local(state, w_qkv, w_out, cotangent, ocean, depth):
    tiles, levs = lax.axis_size("tile"), lax.axis_size("lev")
    plan = Plan(state.shape, tiles, levs)
    height, width, model = plan.height, plan.width, plan.model
    sides = 1 if plan.compact else 2

    def bind(body, *first):
        return lambda *refs: body(*first, *refs)

    def swap(block, axis, first):
        return lax.ppermute(block, axis, swap_pairs(lax.axis_size(axis), first))

    top = height - REACH
    even = lax.rem(lax.axis_index("tile"), 2) == 0
    rows_e = lax.dynamic_slice_in_dim(state, jnp.where(even, top, 0), REACH, 1)
    rows_o = lax.dynamic_slice_in_dim(state, jnp.where(even, 0, top), REACH, 1)
    near = [swap(state, "lev", side) for side in range(sides)]
    rows_e = swap(rows_e, "tile", 0)
    rows_o = swap(rows_o, "tile", 1)
    live = pltpu.SMEM(((plan.levels_n + 2) * plan.tall,), jnp.int32)
    own_cells = plan.own + (model,)
    qs, us, mid = call(
        bind(stage_own, plan),
        "stage_own",
        [(own_cells, BF16), (own_cells, BF16), ((plan.slots_n,) + plan.own[1:] + (2 * model,), BF16)],
        [ocean, depth, state, w_qkv, w_out, cotangent, *near],
        [live],
        cost=4 * 10**9,
    )
    rows_e, rows_o, qs = lax.optimization_barrier((rows_e, rows_o, qs))
    lev_in = []
    for side in range(sides):
        lev_in += [near[side], swap(rows_e, "lev", side), swap(rows_o, "lev", side)]
    rows = model // (tiles * levs)
    if levs == 2 and rows % 8 == 0:
        share = (tiles, rows, 4 * model)
        sums = [(share, F32), (share, BF16)]
    else:
        sums = [((model, 4 * model), F32)]
    keys_n = 3 * (PAIR + 2 * REACH) * width
    attn, dq, dkv16, *sums = call(
        bind(stage_attend, plan, len(sums)),
        "stage_attend",
        [(own_cells, BF16), (own_cells, BF16), (plan.wide + (2 * model,), BF16)] + sums,
        [ocean, depth, state, rows_e, rows_o, qs, us, mid, w_qkv, cotangent, *lev_in],
        [
            pltpu.VMEM(plan.wide + (model,), BF16),
            pltpu.VMEM(plan.wide + (2 * model,), BF16),
            pltpu.VMEM(plan.wide + (2 * model,), F32),
            pltpu.VMEM((keys_n, GROUP * PAIR * width), F32),
            live,
        ],
        mib=24,
        cost=16 * 10**9,
    )
    edge_kind = (plan.wide[1:] + (model,), BF16)
    out, own, part_e, part_o, *edges = call(
        bind(stage_out, plan),
        "stage_out",
        [(own_cells, BF16), (own_cells, F32), (plan.edge, F32), (plan.edge, F32)] + [edge_kind] * sides,
        [state, cotangent, attn, dq, dkv16, w_qkv, w_out],
        [pltpu.VMEM(plan.wide[1:] + (model,), F32)],
        cost=4 * 10**9,
    )
    edges = [swap(edge, "lev", side) for side, edge in enumerate(edges)]
    send_e, send_o = call(
        bind(stage_fold, plan),
        "stage_fold",
        [(plan.edge, BF16)] * 2,
        [part_e, part_o, *edges],
        [pltpu.VMEM(plan.edge, F32)],
    )

    if len(sums) == 2:
        x, parts = sums[0], [lax.ppermute(sums[1], "lev", swap_pairs(levs, 0))]
    else:
        x, parts = reduce_levels(sums[0], tiles, levs), []
    stride = 1
    for radix in digits(tiles):
        share = (x.shape[0] // radix,) + x.shape[1:]
        x, *pieces = call(
            bind(stage_split, len(parts), radix, stride),
            "stage_split",
            [(share, F32)] + [(share, BF16)] * (radix - 1),
            [x, *parts],
        )
        if stride > 1:
            send_e, send_o, *pieces = lax.optimization_barrier((send_e, send_o, *pieces))
        parts = [
            lax.ppermute(piece, "tile", xor_route(tiles, (k + 1) * stride))
            for k, piece in enumerate(pieces)
        ]
        stride *= radix
    d_qkv, d_out = call(
        bind(stage_sum, len(parts)),
        "stage_sum",
        [((rows, 3 * model), F32), ((rows, model), F32)],
        [x, *parts],
    )
    back_e = swap(send_e, "tile", 0)
    back_o = swap(send_o, "tile", 1)
    (d_state,) = call(
        bind(stage_last, plan),
        "stage_last",
        [(own_cells, BF16)],
        [own, back_e, back_o, *edges],
        [pltpu.VMEM(own_cells, F32)],
    )
    return (out, d_state, d_qkv, d_out)


def solution(mesh):
    placed = (P("lev", "tile", None, None), P(), P(), P("lev", "tile", None, None), P(), P())
    return jax.shard_map(
        local,
        mesh=mesh,
        in_specs=placed,
        out_specs=(
            P("lev", "tile", None, None),
            P("lev", "tile", None, None),
            P(("tile", "lev"), None),
            P(("tile", "lev"), None),
        ),
        check_vma=False,
    )
```

```python
import jax
import jax.numpy as jnp
from jax import lax
from jax.experimental import pallas as pl
from jax.experimental.pallas import tpu as pltpu
from jax.sharding import PartitionSpec as P

HEADS = 8
BROWS = 4
REACH = 3
GROUP = 4
PAIR = 2
LOW = -1e30
F32 = jnp.float32
BF16 = jnp.bfloat16
SMEM = pl.BlockSpec(memory_space=pltpu.SMEM)
VMEM = pl.BlockSpec(memory_space=pltpu.VMEM)


def dot(a, b, ca, cb):
    return lax.dot_general(a, b, (((ca,), (cb,)), ((), ())), preferred_element_type=F32)


def swap_pairs(count, first):
    route = []
    for i in range(first, count - 1, 2):
        route += [(i, i + 1), (i + 1, i)]
    return route


def call(body, name, outs, ins, scratch=(), mib=8, cost=10**6):
    return pl.pallas_call(
        body,
        name=name,
        out_shape=[jax.ShapeDtypeStruct(shape, kind) for shape, kind in outs],
        in_specs=[SMEM if x.dtype == jnp.int32 else VMEM for x in ins],
        out_specs=[VMEM] * len(outs),
        scratch_shapes=list(scratch),
        compiler_params=pltpu.CompilerParams(vmem_limit_bytes=mib * 2**20),
        cost_estimate=pl.CostEstimate(flops=cost, bytes_accessed=2**20, transcendentals=0),
    )(*ins)


class Plan:
    def __init__(self, shape, tiles, levs):
        self.levels_n, self.height, self.width, self.model = shape
        self.tiles, self.levs = tiles, levs
        self.tall = self.height + 2 * REACH
        self.compact = levs == 2 and self.levels_n == 2
        self.slots_n = self.levels_n + 2 - self.compact
        self.own = (self.levels_n, self.height, self.width)
        self.wide = (self.slots_n, self.tall, self.width)
        self.edge = (self.levels_n, REACH, self.width, self.model)

    def places(self):
        tile_odd = lax.rem(lax.axis_index("tile"), 2)
        lev_odd = lax.rem(lax.axis_index("lev"), 2)
        end = self.height + REACH
        self.even = tile_odd == 0
        self.at_e = jnp.where(tile_odd == 0, end, 0)
        self.at_o = jnp.where(tile_odd == 0, 0, end)
        self.off = 1 - lev_odd if self.compact else 0
        last = self.levels_n + 1
        self.slot_e = jnp.where(lev_odd == 0, last, 0) - self.off
        self.slot_o = jnp.where(lev_odd == 0, 0, last)
        self.first = 1 - self.off
        self.edge_e = jnp.where(lev_odd == 0, self.levels_n - 1, 0)
        self.edge_o = jnp.where(lev_odd == 0, 0, self.levels_n - 1)

    def liveness(self, ocean, depth, live):
        tile = lax.axis_index("tile")
        lev = lax.axis_index("lev")
        total_rows = self.height * self.tiles
        total_levels = self.levels_n * self.levs
        for r in range(self.tall):
            row = tile * self.height - REACH + r
            block_at = lax.div(jnp.clip(row, 0, total_rows - 1), BROWS)
            good = (row >= 0) & (row < total_rows) & (ocean[block_at] == 1)
            deep = depth[block_at]
            for l in range(self.levels_n + 2):
                at = lev * self.levels_n - 1 + l
                ok = good & (at >= 0) & (at < total_levels) & (at < deep)
                live[l * self.tall + r] = ok.astype(jnp.int32)

    def alive(self, live, level, row):
        return live[level * self.tall + row]


def stage_own(plan, ocean, depth, state, w_qkv, w_out, cot, *refs):
    near, (qs, us, mid, live) = refs[:-4], refs[-4:]
    height, width, model = plan.own[1:] + (plan.model,)
    cells = height * width
    head = model // HEADS
    plan.places()
    plan.liveness(ocean, depth, live)

    def pairs(x):
        y = dot(x.reshape(cells, model), w_qkv[:, model:], 1, 0).astype(BF16)
        return y.reshape(height, width, 2 * model)

    for l in range(plan.levels_n):
        mid[plan.first + l] = pairs(state[l])
        flat = state[l].reshape(cells, model)
        q = dot(flat, w_qkv[:, :model], 1, 0).astype(BF16) * jnp.asarray(head**-0.5, BF16)
        qs[l] = q.reshape(height, width, model)
        u = dot(cot[l].reshape(cells, model), w_out[...], 1, 1).astype(BF16)
        u = u.reshape(height, width, model)
        for r in range(height):
            us[l, r] = u[r] * plan.alive(live, l + 1, REACH + r).astype(F32).astype(BF16)
    mid[plan.slot_e] = pairs(near[0][plan.edge_o])
    if not plan.compact:
        mid[plan.slot_o] = pairs(near[1][plan.edge_e])


def stage_attend(plan, sums_n, ocean, depth, state, rows_e, rows_o, qs, us, mid, w_qkv, cot, *refs):
    sides = 1 if plan.compact else 2
    lev_in, refs = refs[: 3 * sides], refs[3 * sides :]
    attn, dq, dkv16 = refs[:3]
    sums, (ext, kv, dkv, bias, live) = refs[3 : 3 + sums_n], refs[3 + sums_n :]
    levels_n, height, width = plan.own
    model, tall = plan.model, plan.tall
    span = PAIR + 2 * REACH
    block = PAIR * width
    head = model // HEADS
    lanes_n = GROUP * head
    plan.places()
    plan.liveness(ocean, depth, live)

    inner = pl.ds(plan.first, levels_n)
    ext[inner, REACH : height + REACH] = state[...]
    ext[inner, pl.ds(plan.at_e, REACH)] = rows_e[...]
    ext[inner, pl.ds(plan.at_o, REACH)] = rows_o[...]
    for side, (slot, level) in enumerate(((plan.slot_e, plan.edge_o), (plan.slot_o, plan.edge_e))):
        if side < sides:
            near, far_e, far_o = lev_in[3 * side : 3 * side + 3]
            ext[slot, REACH : height + REACH] = near[level]
            ext[slot, pl.ds(plan.at_e, REACH)] = far_e[level]
            ext[slot, pl.ds(plan.at_o, REACH)] = far_o[level]

    @pl.loop(0, plan.slots_n)
    def _(l):
        edge = REACH * width
        cells = [ext[l, :REACH].reshape(edge, model), ext[l, height + REACH :].reshape(edge, model)]
        pairs = dot(jnp.concatenate(cells, axis=0), w_qkv[:, model:], 1, 0).astype(BF16)
        kv[l, :REACH] = pairs[:edge].reshape(REACH, width, 2 * model)
        kv[l, height + REACH :] = pairs[edge:].reshape(REACH, width, 2 * model)
        kv[l, REACH : height + REACH] = mid[l]
        dkv[l] = jnp.zeros((tall, width, 2 * model), F32)

    lane_head = lax.broadcasted_iota(jnp.int32, (block, lanes_n), 1) // head
    query = lax.broadcasted_iota(jnp.int32, (width, GROUP * block), 1) % block
    query_row = query // width
    query_col = query % width
    key_col = lax.broadcasted_iota(jnp.int32, (width, GROUP * block), 0)
    near_col = jnp.abs(key_col - query_col) <= REACH

    def spread(x):
        return jnp.concatenate(
            [jnp.where(lane_head == h, x, jnp.zeros_like(x)) for h in range(GROUP)], axis=0
        )

    def gather(x):
        total = jnp.where(lane_head == 0, x[:block], 0.0)
        for h in range(1, GROUP):
            total = jnp.where(lane_head == h, x[h * block : (h + 1) * block], total)
        return total

    def tile_step(l, r0, depth_n, base, base_level):
        keys_n = depth_n * span * width
        for dl in range(depth_n):
            for kr in range(span):
                alive = plan.alive(live, base_level + dl, r0 + kr) == 1
                near = near_col & (jnp.abs(query_row + REACH - kr) <= REACH)
                at = (dl * span + kr) * width
                bias[at : at + width] = jnp.where(near & alive, 0.0, LOW)
        for g in range(HEADS // GROUP):
            lanes = slice(g * lanes_n, (g + 1) * lanes_n)
            lanes_v = slice(model + g * lanes_n, model + (g + 1) * lanes_n)
            q = spread(qs[l, pl.ds(r0, PAIR), :, lanes].reshape(block, lanes_n))
            u = spread(us[l, pl.ds(r0, PAIR), :, lanes].reshape(block, lanes_n))
            k = kv[pl.ds(base, depth_n), pl.ds(r0, span), :, lanes].reshape(keys_n, lanes_n)
            v = kv[pl.ds(base, depth_n), pl.ds(r0, span), :, lanes_v].reshape(keys_n, lanes_n)
            s = dot(k, q, 1, 1) + bias[:keys_n]
            e = jnp.exp(s - jnp.max(s, axis=0, keepdims=True))
            p = e * (1.0 / jnp.sum(e, axis=0, keepdims=True))
            p16 = p.astype(BF16)
            dp = dot(v, u, 1, 1)
            ds = p * (dp - jnp.sum(p * dp, axis=0, keepdims=True))
            ds16 = ds.astype(BF16)
            a = gather(dot(p16, v, 0, 0))
            for r in range(PAIR):
                alive = plan.alive(live, l + 1, REACH + r0 + r).astype(F32)
                attn[l, r0 + r, :, lanes] = (a[r * width : (r + 1) * width] * alive).astype(BF16)
            b = gather(dot(ds16, k, 0, 0)) * (head**-0.5)
            dq[l, pl.ds(r0, PAIR), :, lanes] = b.astype(BF16).reshape(PAIR, width, lanes_n)
            dk = dot(ds16, q, 1, 0).reshape(depth_n, span, width, lanes_n)
            dkv[pl.ds(base, depth_n), pl.ds(r0, span), :, lanes] += dk
            dv = dot(p16, u, 1, 0).reshape(depth_n, span, width, lanes_n)
            dkv[pl.ds(base, depth_n), pl.ds(r0, span), :, lanes_v] += dv

    pairs_n = height // PAIR
    if plan.compact:

        @pl.loop(0, pairs_n)
        def _(pair):
            tile_step(plan.edge_e, pair * PAIR, 3, 0, plan.off)
            tile_step(plan.edge_o, pair * PAIR, 2, plan.first, 1)

    else:

        @pl.loop(0, levels_n * pairs_n)
        def _(combo):
            l = combo // pairs_n
            tile_step(l, (combo % pairs_n) * PAIR, 3, l, l)

    @pl.loop(0, plan.slots_n)
    def _(l):
        dkv16[l] = dkv[l].astype(BF16)

    cells = levels_n * height * width
    wide = plan.slots_n * tall * width

    def emit(at, x):
        n = x.shape[1]
        if sums_n == 1:
            sums[0][:, at : at + n] = x
            return
        keep, send = sums
        rows = model // (plan.tiles * plan.levs)
        x = x.reshape(plan.tiles, plan.levs, rows, n)
        mine = lax.axis_index("lev") == 0
        keep[:, :, at : at + n] = jnp.where(mine, x[:, 0], x[:, 1])
        send[:, :, at : at + n] = jnp.where(mine, x[:, 1], x[:, 0]).astype(BF16)

    emit(0, dot(state[...].reshape(cells, model), dq[...].reshape(cells, model), 0, 0))
    emit(3 * model, dot(attn[...].reshape(cells, model), cot[...].reshape(cells, model), 0, 0))
    for j in range(2):
        part = dkv16[:, :, :, j * model : (j + 1) * model].reshape(wide, model)
        emit((j + 1) * model, dot(ext[...].reshape(wide, model), part, 0, 0))


def stage_out(plan, state, cot, attn, dq, dkv16, w_qkv, w_out, out, own, rows_e, rows_o, *refs):
    edges, tmp = refs[:-1], refs[-1]
    levels_n, height, width = plan.own
    model, tall = plan.model, plan.tall
    cells = height * width
    plan.places()

    def back(slot):
        x = dot(dkv16[slot].reshape(tall * width, 2 * model), w_qkv[:, model:], 1, 1)
        return x.reshape(tall, width, model)

    for edge, slot in zip(edges, (plan.slot_e, plan.slot_o)):
        edge[...] = back(slot).astype(BF16)
    for l in range(levels_n):
        tmp[...] = back(plan.first + l)
        rows_e[l] = tmp[pl.ds(plan.at_e, REACH)]
        rows_o[l] = tmp[pl.ds(plan.at_o, REACH)]
        x = cot[l].reshape(cells, model).astype(F32)
        x = x + dot(dq[l].reshape(cells, model), w_qkv[:, :model], 1, 1)
        own[l] = x.reshape(height, width, model) + tmp[REACH : REACH + height]
        x = state[l].reshape(cells, model).astype(F32)
        x = x + dot(attn[l].reshape(cells, model), w_out[...], 1, 0)
        out[l] = x.astype(BF16).reshape(height, width, model)


def stage_fold(plan, rows_e, rows_o, *refs):
    edges, (send_e, send_o, acc) = refs[:-3], refs[-3:]
    plan.places()
    for rows, at, send in ((rows_e, plan.at_e, send_e), (rows_o, plan.at_o, send_o)):
        acc[...] = rows[...]
        for edge, level in zip(edges, (plan.edge_e, plan.edge_o)):
            acc[level] += edge[pl.ds(at, REACH)].astype(F32)
        send[...] = acc[...].astype(BF16)


def stage_last(plan, own, back_e, back_o, *refs):
    edges, (d_state, acc) = refs[:-2], refs[-2:]
    plan.places()
    height = plan.height
    acc[...] = own[...]
    for edge, level in zip(edges, (plan.edge_e, plan.edge_o)):
        acc[level] += edge[REACH : REACH + height].astype(F32)
    top = height - REACH
    acc[:, pl.ds(jnp.where(plan.even, top, 0), REACH)] += back_e[...].astype(F32)
    acc[:, pl.ds(jnp.where(plan.even, 0, top), REACH)] += back_o[...].astype(F32)
    d_state[...] = acc[...].astype(BF16)


def stage_split(parts_n, radix, stride, x, *refs):
    parts, (own, *pieces) = refs[:parts_n], refs[parts_n:]
    digit = lax.rem(lax.div(lax.axis_index("tile"), stride), radix)
    for h in range(x.shape[0] // radix):
        for k in range(radix):
            at = h * radix + jnp.bitwise_xor(digit, k)
            y = x[at]
            for part in parts:
                y = y + part[at].astype(F32)
            if k == 0:
                own[h] = y
            else:
                pieces[k - 1][h] = y.astype(BF16)


def stage_sum(parts_n, x, *refs):
    parts, (qkv, rest) = refs[:parts_n], refs[parts_n:]
    y = x[0]
    for part in parts:
        y = y + part[0].astype(F32)
    cut = qkv.shape[1]
    qkv[...] = y[:, :cut]
    rest[...] = y[:, cut:]


def digits(count):
    sizes = []
    while count > 1:
        radix = 4 if count % 4 == 0 else 2
        sizes.append(radix)
        count //= radix
    return sizes


def xor_route(count, step):
    return [(i, i ^ step) for i in range(count)]


def reduce_levels(x, tiles, levs):
    rows, cols = x.shape
    x = x.reshape([tiles] + digits(levs)[::-1] + [rows // (tiles * levs), cols])
    stride = 1
    for radix in digits(levs):
        dim = x.ndim - 3
        digit = lax.rem(lax.div(lax.axis_index("lev"), stride), radix)
        total = lax.dynamic_index_in_dim(x, digit, dim, keepdims=False)
        for k in range(1, radix):
            piece = lax.dynamic_index_in_dim(x, jnp.bitwise_xor(digit, k), dim, keepdims=False)
            piece = lax.ppermute(piece.astype(BF16), "lev", xor_route(levs, k * stride))
            total = total + piece.astype(F32)
        x = total
        stride *= radix
    return x


def local(state, w_qkv, w_out, cotangent, ocean, depth):
    tiles, levs = lax.axis_size("tile"), lax.axis_size("lev")
    plan = Plan(state.shape, tiles, levs)
    height, width, model = plan.height, plan.width, plan.model
    sides = 1 if plan.compact else 2

    def bind(body, *first):
        return lambda *refs: body(*first, *refs)

    def swap(block, axis, first):
        return lax.ppermute(block, axis, swap_pairs(lax.axis_size(axis), first))

    top = height - REACH
    even = lax.rem(lax.axis_index("tile"), 2) == 0
    rows_e = lax.dynamic_slice_in_dim(state, jnp.where(even, top, 0), REACH, 1)
    rows_o = lax.dynamic_slice_in_dim(state, jnp.where(even, 0, top), REACH, 1)
    near = [swap(state, "lev", side) for side in range(sides)]
    rows_e = swap(rows_e, "tile", 0)
    rows_o = swap(rows_o, "tile", 1)
    live = pltpu.SMEM(((plan.levels_n + 2) * plan.tall,), jnp.int32)
    own_cells = plan.own + (model,)
    qs, us, mid = call(
        bind(stage_own, plan),
        "stage_own",
        [(own_cells, BF16), (own_cells, BF16), ((plan.slots_n,) + plan.own[1:] + (2 * model,), BF16)],
        [ocean, depth, state, w_qkv, w_out, cotangent, *near],
        [live],
        cost=4 * 10**9,
    )
    rows_e, rows_o, qs = lax.optimization_barrier((rows_e, rows_o, qs))
    lev_in = []
    for side in range(sides):
        lev_in += [near[side], swap(rows_e, "lev", side), swap(rows_o, "lev", side)]
    rows = model // (tiles * levs)
    if levs == 2 and rows % 8 == 0:
        share = (tiles, rows, 4 * model)
        sums = [(share, F32), (share, BF16)]
    else:
        sums = [((model, 4 * model), F32)]
    keys_n = 3 * (PAIR + 2 * REACH) * width
    attn, dq, dkv16, *sums = call(
        bind(stage_attend, plan, len(sums)),
        "stage_attend",
        [(own_cells, BF16), (own_cells, BF16), (plan.wide + (2 * model,), BF16)] + sums,
        [ocean, depth, state, rows_e, rows_o, qs, us, mid, w_qkv, cotangent, *lev_in],
        [
            pltpu.VMEM(plan.wide + (model,), BF16),
            pltpu.VMEM(plan.wide + (2 * model,), BF16),
            pltpu.VMEM(plan.wide + (2 * model,), F32),
            pltpu.VMEM((keys_n, GROUP * PAIR * width), F32),
            live,
        ],
        mib=24,
        cost=16 * 10**9,
    )
    edge_kind = (plan.wide[1:] + (model,), BF16)
    out, own, part_e, part_o, *edges = call(
        bind(stage_out, plan),
        "stage_out",
        [(own_cells, BF16), (own_cells, F32), (plan.edge, F32), (plan.edge, F32)] + [edge_kind] * sides,
        [state, cotangent, attn, dq, dkv16, w_qkv, w_out],
        [pltpu.VMEM(plan.wide[1:] + (model,), F32)],
        cost=4 * 10**9,
    )
    edges = [swap(edge, "lev", side) for side, edge in enumerate(edges)]
    send_e, send_o = call(
        bind(stage_fold, plan),
        "stage_fold",
        [(plan.edge, BF16)] * 2,
        [part_e, part_o, *edges],
        [pltpu.VMEM(plan.edge, F32)],
    )

    if len(sums) == 2:
        x, parts = sums[0], [lax.ppermute(sums[1], "lev", swap_pairs(levs, 0))]
    else:
        x, parts = reduce_levels(sums[0], tiles, levs), []
    stride = 1
    for radix in digits(tiles):
        share = (x.shape[0] // radix,) + x.shape[1:]
        x, *pieces = call(
            bind(stage_split, len(parts), radix, stride),
            "stage_split",
            [(share, F32)] + [(share, BF16)] * (radix - 1),
            [x, *parts],
        )
        parts = [
            lax.ppermute(piece, "tile", xor_route(tiles, (k + 1) * stride))
            for k, piece in enumerate(pieces)
        ]
        if stride == 1:
            send_e, send_o, parts[2] = lax.optimization_barrier((send_e, send_o, parts[2]))
        stride *= radix
    d_qkv, d_out = call(
        bind(stage_sum, len(parts)),
        "stage_sum",
        [((rows, 3 * model), F32), ((rows, model), F32)],
        [x, *parts],
    )
    back_e = swap(send_e, "tile", 0)
    back_o = swap(send_o, "tile", 1)
    (d_state,) = call(
        bind(stage_last, plan),
        "stage_last",
        [(own_cells, BF16)],
        [own, back_e, back_o, *edges],
        [pltpu.VMEM(own_cells, F32)],
    )
    return (out, d_state, d_qkv, d_out)


def solution(mesh):
    placed = (P("lev", "tile", None, None), P(), P(), P("lev", "tile", None, None), P(), P())
    return jax.shard_map(
        local,
        mesh=mesh,
        in_specs=placed,
        out_specs=(
            P("lev", "tile", None, None),
            P("lev", "tile", None, None),
            P(("tile", "lev"), None),
            P(("tile", "lev"), None),
        ),
        check_vma=False,
    )
```

```python
import jax
import jax.numpy as jnp
from jax import lax
from jax.experimental import pallas as pl
from jax.experimental.pallas import tpu as pltpu
from jax.sharding import PartitionSpec as P

HEADS = 8
BROWS = 4
REACH = 3
GROUP = 4
PAIR = 2
LOW = -1e30
F32 = jnp.float32
BF16 = jnp.bfloat16
SMEM = pl.BlockSpec(memory_space=pltpu.SMEM)
VMEM = pl.BlockSpec(memory_space=pltpu.VMEM)


def dot(a, b, ca, cb):
    return lax.dot_general(a, b, (((ca,), (cb,)), ((), ())), preferred_element_type=F32)


def swap_pairs(count, first):
    route = []
    for i in range(first, count - 1, 2):
        route += [(i, i + 1), (i + 1, i)]
    return route


def call(body, name, outs, ins, scratch=(), mib=8, cost=10**6, aliases={}):
    return pl.pallas_call(
        body,
        name=name,
        out_shape=[jax.ShapeDtypeStruct(shape, kind) for shape, kind in outs],
        in_specs=[SMEM if x.dtype == jnp.int32 else VMEM for x in ins],
        out_specs=[VMEM] * len(outs),
        scratch_shapes=list(scratch),
        compiler_params=pltpu.CompilerParams(vmem_limit_bytes=mib * 2**20),
        input_output_aliases=aliases,
        cost_estimate=pl.CostEstimate(flops=cost, bytes_accessed=2**20, transcendentals=0),
    )(*ins)


class Plan:
    def __init__(self, shape, tiles, levs):
        self.levels_n, self.height, self.width, self.model = shape
        self.tiles, self.levs = tiles, levs
        self.tall = self.height + 2 * REACH
        self.compact = levs == 2 and self.levels_n == 2 and self.height == 2 * PAIR
        self.blocks_n = self.levels_n * self.height // PAIR
        self.lanes_n = GROUP * self.model // HEADS
        self.queries_n = GROUP * PAIR * self.width
        self.slots_n = self.levels_n + 2 - self.compact
        self.own = (self.levels_n, self.height, self.width)
        self.wide = (self.slots_n, self.tall, self.width)
        self.edge = (self.levels_n, REACH, self.width, self.model)

    def places(self):
        tile_odd = lax.rem(lax.axis_index("tile"), 2)
        lev_odd = lax.rem(lax.axis_index("lev"), 2)
        end = self.height + REACH
        self.even = tile_odd == 0
        self.at_e = jnp.where(tile_odd == 0, end, 0)
        self.at_o = jnp.where(tile_odd == 0, 0, end)
        self.off = 1 - lev_odd if self.compact else 0
        last = self.levels_n + 1
        self.slot_e = jnp.where(lev_odd == 0, last, 0) - self.off
        self.slot_o = jnp.where(lev_odd == 0, 0, last)
        self.first = 1 - self.off
        self.edge_e = jnp.where(lev_odd == 0, self.levels_n - 1, 0)
        self.edge_o = jnp.where(lev_odd == 0, 0, self.levels_n - 1)
        if self.compact:
            far = [(self.edge_o, r0, 2, self.first, 1) for r0 in (0, PAIR)]
            near = [(self.edge_e, r0, 3, 0, self.off) for r0 in (0, PAIR)]
            self.blocks = [far[0], near[0], near[1], far[1]]
        else:
            rows = range(0, self.height, PAIR)
            self.blocks = [(l, r0, 3, l, l) for l in range(self.levels_n) for r0 in rows]

    def liveness(self, ocean, depth, live):
        tile = lax.axis_index("tile")
        lev = lax.axis_index("lev")
        total_rows = self.height * self.tiles
        total_levels = self.levels_n * self.levs
        for r in range(self.tall):
            row = tile * self.height - REACH + r
            block_at = lax.div(jnp.clip(row, 0, total_rows - 1), BROWS)
            good = (row >= 0) & (row < total_rows) & (ocean[block_at] == 1)
            deep = depth[block_at]
            for l in range(self.levels_n + 2):
                at = lev * self.levels_n - 1 + l
                ok = good & (at >= 0) & (at < total_levels) & (at < deep)
                live[l * self.tall + r] = ok.astype(jnp.int32)

    def alive(self, live, level, row):
        return live[level * self.tall + row]


def stage_cut(plan, state, rows_e, rows_o, sems):
    top = plan.height - REACH
    plan.places()
    at_e, at_o = jnp.where(plan.even, top, 0), jnp.where(plan.even, 0, top)
    cut_e = pltpu.make_async_copy(state.at[:, pl.ds(at_e, REACH)], rows_e, sems.at[0])
    cut_o = pltpu.make_async_copy(state.at[:, pl.ds(at_o, REACH)], rows_o, sems.at[1])
    cut_e.start()
    cut_o.start()
    cut_e.wait()
    cut_o.wait()


def stage_own(plan, ocean, depth, state, w_qkv, w_out, cot, *refs):
    near, (qs, us, mid, live) = refs[:-4], refs[-4:]
    height, width, model = plan.own[1:] + (plan.model,)
    cells = height * width
    head = model // HEADS
    plan.places()
    plan.liveness(ocean, depth, live)

    def pairs(x):
        y = dot(x.reshape(cells, model), w_qkv[:, model:], 1, 0).astype(BF16)
        return y.reshape(height, width, 2 * model)

    for l in range(plan.levels_n):
        mid[plan.first + l] = pairs(state[l])
        flat = state[l].reshape(cells, model)
        q = dot(flat, w_qkv[:, :model], 1, 0).astype(BF16) * jnp.asarray(head**-0.5, BF16)
        qs[l] = q.reshape(height, width, model)
        u = dot(cot[l].reshape(cells, model), w_out[...], 1, 1).astype(BF16)
        u = u.reshape(height, width, model)
        for r in range(height):
            us[l, r] = u[r] * plan.alive(live, l + 1, REACH + r).astype(F32).astype(BF16)
    mid[plan.slot_e] = pairs(near[0][plan.edge_o])
    if not plan.compact:
        mid[plan.slot_o] = pairs(near[1][plan.edge_e])


def spread(plan, x):
    lane_head = lax.broadcasted_iota(jnp.int32, x.shape, 1) // (plan.model // HEADS)
    return jnp.concatenate(
        [jnp.where(lane_head == h, x, jnp.zeros_like(x)) for h in range(GROUP)], axis=0
    )


def group_lanes(plan, g):
    lanes = slice(g * plan.lanes_n, (g + 1) * plan.lanes_n)
    return lanes, slice(plan.model + lanes.start, plan.model + lanes.stop)


def spread_block(plan, x, block, lanes):
    l, r0 = block[:2]
    return spread(plan, x[l, r0 : r0 + PAIR, :, lanes].reshape(PAIR * plan.width, plan.lanes_n))


def attention(plan, numbers, live, qs, us, kv, bias, prob, grad, attn, dq):
    width, lanes_n, queries_n = plan.width, plan.lanes_n, plan.queries_n
    span = PAIR + 2 * REACH
    block_n = PAIR * width
    head = plan.model // HEADS
    lane_head = lax.broadcasted_iota(jnp.int32, (block_n, lanes_n), 1) // head
    query = lax.broadcasted_iota(jnp.int32, (width, queries_n), 1) % block_n
    query_row = query // width
    query_col = query % width
    key_col = lax.broadcasted_iota(jnp.int32, (width, queries_n), 0)
    near_col = jnp.abs(key_col - query_col) <= REACH

    def gather(x):
        total = jnp.where(lane_head == 0, x[:block_n], 0.0)
        for h in range(1, GROUP):
            total = jnp.where(lane_head == h, x[h * block_n : (h + 1) * block_n], total)
        return total

    def scores(slot, number, g):
        block = plan.blocks[number]
        l, r0, depth_n, base, _ = block
        keys_n = depth_n * span * width
        lanes, lanes_v = group_lanes(plan, g)
        q = spread_block(plan, qs, block, lanes)
        u = spread_block(plan, us, block, lanes)
        k = kv[pl.ds(base, depth_n), r0 : r0 + span, :, lanes].reshape(keys_n, lanes_n)
        v = kv[pl.ds(base, depth_n), r0 : r0 + span, :, lanes_v].reshape(keys_n, lanes_n)
        return k, v, dot(k, q, 1, 1) + bias[slot, :keys_n], dot(v, u, 1, 1)

    def weigh(s, dp):
        e = jnp.exp(s - jnp.max(s, axis=0, keepdims=True))
        inv = 1.0 / jnp.sum(e, axis=0, keepdims=True)
        delta = jnp.sum(e * dp, axis=0, keepdims=True) * inv
        p = e * inv
        return p.astype(BF16), (p * (dp - delta)).astype(BF16)

    def give(number, g, p16, ds16, k, v):
        l, r0, depth_n, base, _ = plan.blocks[number]
        lanes = group_lanes(plan, g)[0]
        at = slice(number * queries_n, (number + 1) * queries_n)
        tiled = (depth_n, span, width, queries_n)
        prob[g, pl.ds(base, depth_n), r0 : r0 + span, :, at] = p16.reshape(tiled)
        grad[g, pl.ds(base, depth_n), r0 : r0 + span, :, at] = ds16.reshape(tiled)
        a = gather(dot(p16, v, 0, 0))
        for r in range(PAIR):
            alive = plan.alive(live, l + 1, REACH + r0 + r).astype(F32)
            attn[l, r0 + r, :, lanes] = (a[r * width : (r + 1) * width] * alive).astype(BF16)
        b = gather(dot(ds16, k, 0, 0)) * (head**-0.5)
        dq[l, r0 : r0 + PAIR, :, lanes] = b.astype(BF16).reshape(PAIR, width, lanes_n)

    def mask(slot, number):
        _, r0, depth_n, _, base_level = plan.blocks[number]
        for dl in range(depth_n):
            for kr in range(span):
                alive = plan.alive(live, base_level + dl, r0 + kr) == 1
                near = near_col & (jnp.abs(query_row + REACH - kr) <= REACH)
                at = (dl * span + kr) * width
                bias[slot, at : at + width] = jnp.where(near & alive, 0.0, LOW)

    jobs = []
    for i, number in enumerate(numbers):
        mask(i, number)
        jobs += [(i, number, g) for g in range(HEADS // GROUP)]
    ready = [scores(*jobs[0])]
    for i, job in enumerate(jobs):
        if i + 1 < len(jobs):
            ready.append(scores(*jobs[i + 1]))
        k, v, s, dp = ready[i]
        give(*job[1:], *weigh(s, dp), k, v)


def sum_keys(plan, qs, us, prob, grad, dkv16):
    n = plan.queries_n
    if plan.compact:
        own, edge = pl.ds(plan.first, plan.levels_n), pl.ds(plan.slot_e, 1)
        end = plan.tall
        parts = [(own, plan.levels_n, 0, PAIR, 0, 2), (own, plan.levels_n, PAIR, end - PAIR, 0, 4)]
        parts += [(own, plan.levels_n, end - PAIR, end, 2, 4), (edge, 1, 0, PAIR, 1, 2)]
        parts += [(edge, 1, PAIR, end - PAIR, 1, 3), (edge, 1, end - PAIR, end, 2, 3)]
    else:
        parts = [(pl.ds(i, 1), 1, 0, plan.tall, 0, plan.blocks_n) for i in range(plan.slots_n)]
    for g in range(HEADS // GROUP):
        lanes, lanes_v = group_lanes(plan, g)
        for source, weights, at in ((qs, grad, lanes), (us, prob, lanes_v)):
            x = [spread_block(plan, source, block, lanes) for block in plan.blocks]
            x = jnp.concatenate(x, axis=0)
            for slots, slots_n, low, high, k0, k1 in parts:
                w = weights[g, slots, low:high, :, k0 * n : k1 * n]
                w = w.reshape(slots_n * (high - low) * plan.width, (k1 - k0) * n)
                y = dot(w, x[k0 * n : k1 * n], 1, 0).astype(BF16)
                dkv16[slots, low:high, :, at] = y.reshape(slots_n, high - low, plan.width, plan.lanes_n)


def project(plan, slot, ext, mid, w_qkv, kv):
    height, width = plan.own[1:]
    model = plan.model
    edge = REACH * width
    cells = [ext[slot, :REACH].reshape(edge, model), ext[slot, height + REACH :].reshape(edge, model)]
    pairs = dot(jnp.concatenate(cells, axis=0), w_qkv[:, model:], 1, 0).astype(BF16)
    kv[slot, :REACH] = pairs[:edge].reshape(REACH, width, 2 * model)
    kv[slot, height + REACH :] = pairs[edge:].reshape(REACH, width, 2 * model)
    kv[slot, REACH : height + REACH] = mid[slot]


def stage_inner(plan, ocean, depth, state, rows_e, rows_o, qs, us, mid, w_qkv, *refs):
    ext, kv, prob, grad, attn, dq, bias, live = refs
    levels_n, height = plan.own[:2]
    plan.places()
    plan.liveness(ocean, depth, live)
    inner = pl.ds(plan.first, levels_n)
    ext[inner, REACH : height + REACH] = state[...]
    ext[inner, pl.ds(plan.at_e, REACH)] = rows_e[...]
    ext[inner, pl.ds(plan.at_o, REACH)] = rows_o[...]
    for l in range(levels_n):
        project(plan, plan.first + l, ext, mid, w_qkv, kv)
    if plan.compact:
        attention(plan, (0, 3), live, qs, us, kv, bias, prob, grad, attn, dq)


def stage_attend(plan, sums_n, ocean, depth, state, qs, us, mid, w_qkv, cot, *refs):
    sides = 1 if plan.compact else 2
    lev_in, refs = refs[: 3 * sides], refs[3 * sides + 6 :]
    ext, kv, prob, grad, attn, dq, dkv16 = refs[:7]
    sums, (bias, live) = refs[7 : 7 + sums_n], refs[7 + sums_n :]
    levels_n, height, width = plan.own
    model, tall = plan.model, plan.tall
    plan.places()
    plan.liveness(ocean, depth, live)
    for side, (slot, level) in enumerate(((plan.slot_e, plan.edge_o), (plan.slot_o, plan.edge_e))):
        if side < sides:
            near, far_e, far_o = lev_in[3 * side : 3 * side + 3]
            ext[slot, REACH : height + REACH] = near[level]
            ext[slot, pl.ds(plan.at_e, REACH)] = far_e[level]
            ext[slot, pl.ds(plan.at_o, REACH)] = far_o[level]
            project(plan, slot, ext, mid, w_qkv, kv)
    if plan.compact:
        numbers = (1, 2)
    else:
        numbers = range(plan.blocks_n)
        prob[...] = jnp.zeros(prob.shape, BF16)
        grad[...] = jnp.zeros(grad.shape, BF16)
    attention(plan, numbers, live, qs, us, kv, bias, prob, grad, attn, dq)
    sum_keys(plan, qs, us, prob, grad, dkv16)
    cells = levels_n * height * width
    wide = plan.slots_n * tall * width

    def emit(at, x):
        n = x.shape[1]
        if sums_n == 1:
            sums[0][:, at : at + n] = x
            return
        keep, send = sums
        rows = model // (plan.tiles * plan.levs)
        x = x.reshape(plan.tiles, plan.levs, rows, n)
        mine = lax.axis_index("lev") == 0
        keep[:, :, at : at + n] = jnp.where(mine, x[:, 0], x[:, 1])
        send[:, :, at : at + n] = jnp.where(mine, x[:, 1], x[:, 0]).astype(BF16)

    emit(0, dot(state[...].reshape(cells, model), dq[...].reshape(cells, model), 0, 0))
    emit(3 * model, dot(attn[...].reshape(cells, model), cot[...].reshape(cells, model), 0, 0))
    for j in range(2):
        part = dkv16[:, :, :, j * model : (j + 1) * model].reshape(wide, model)
        emit((j + 1) * model, dot(ext[...].reshape(wide, model), part, 0, 0))


def stage_out(plan, state, cot, attn, dq, dkv16, w_qkv, w_out, out, own, rows_e, rows_o, *refs):
    edges, tmp = refs[:-1], refs[-1]
    levels_n, height, width = plan.own
    model, tall = plan.model, plan.tall
    cells = height * width
    plan.places()

    def back(slot):
        x = dot(dkv16[slot].reshape(tall * width, 2 * model), w_qkv[:, model:], 1, 1)
        return x.reshape(tall, width, model)

    for edge, slot in zip(edges, (plan.slot_e, plan.slot_o)):
        edge[...] = back(slot).astype(BF16)
    for l in range(levels_n):
        tmp[...] = back(plan.first + l)
        rows_e[l] = tmp[pl.ds(plan.at_e, REACH)]
        rows_o[l] = tmp[pl.ds(plan.at_o, REACH)]
        x = cot[l].reshape(cells, model).astype(F32)
        x = x + dot(dq[l].reshape(cells, model), w_qkv[:, :model], 1, 1)
        own[l] = x.reshape(height, width, model) + tmp[REACH : REACH + height]
        x = state[l].reshape(cells, model).astype(F32)
        x = x + dot(attn[l].reshape(cells, model), w_out[...], 1, 0)
        out[l] = x.astype(BF16).reshape(height, width, model)


def stage_fold(plan, rows_e, rows_o, *refs):
    edges, (send_e, send_o, acc) = refs[:-3], refs[-3:]
    plan.places()
    for rows, at, send in ((rows_e, plan.at_e, send_e), (rows_o, plan.at_o, send_o)):
        acc[...] = rows[...]
        for edge, level in zip(edges, (plan.edge_e, plan.edge_o)):
            acc[level] += edge[pl.ds(at, REACH)].astype(F32)
        send[...] = acc[...].astype(BF16)


def stage_last(plan, parts_n, own, back_e, back_o, x, *refs):
    parts, edges, (d_state, d_qkv, d_out, acc) = refs[:parts_n], refs[parts_n:-4], refs[-4:]
    plan.places()
    height = plan.height
    acc[...] = own[...]
    for edge, level in zip(edges, (plan.edge_e, plan.edge_o)):
        acc[level] += edge[REACH : REACH + height].astype(F32)
    top = height - REACH
    acc[:, pl.ds(jnp.where(plan.even, top, 0), REACH)] += back_e[...].astype(F32)
    acc[:, pl.ds(jnp.where(plan.even, 0, top), REACH)] += back_o[...].astype(F32)
    d_state[...] = acc[...].astype(BF16)
    y = x[0]
    for part in parts:
        y = y + part[0].astype(F32)
    cut = d_qkv.shape[1]
    d_qkv[...] = y[:, :cut]
    d_out[...] = y[:, cut:]


def stage_split(parts_n, radix, stride, x, *refs):
    parts, (own, *pieces) = refs[:parts_n], refs[parts_n:]
    digit = lax.rem(lax.div(lax.axis_index("tile"), stride), radix)
    for h in range(x.shape[0] // radix):
        for k in range(radix):
            at = h * radix + jnp.bitwise_xor(digit, k)
            y = x[at]
            for part in parts:
                y = y + part[at].astype(F32)
            if k == 0:
                own[h] = y
            else:
                pieces[k - 1][h] = y.astype(BF16)


def digits(count):
    sizes = []
    while count > 1:
        radix = 4 if count % 4 == 0 else 2
        sizes.append(radix)
        count //= radix
    return sizes


def xor_route(count, step):
    return [(i, i ^ step) for i in range(count)]


def reduce_levels(x, tiles, levs):
    rows, cols = x.shape
    x = x.reshape([tiles] + digits(levs)[::-1] + [rows // (tiles * levs), cols])
    stride = 1
    for radix in digits(levs):
        dim = x.ndim - 3
        digit = lax.rem(lax.div(lax.axis_index("lev"), stride), radix)
        total = lax.dynamic_index_in_dim(x, digit, dim, keepdims=False)
        for k in range(1, radix):
            piece = lax.dynamic_index_in_dim(x, jnp.bitwise_xor(digit, k), dim, keepdims=False)
            piece = lax.ppermute(piece.astype(BF16), "lev", xor_route(levs, k * stride))
            total = total + piece.astype(F32)
        x = total
        stride *= radix
    return x


def local(state, w_qkv, w_out, cotangent, ocean, depth):
    tiles, levs = lax.axis_size("tile"), lax.axis_size("lev")
    plan = Plan(state.shape, tiles, levs)
    height, width, model = plan.height, plan.width, plan.model
    sides = 1 if plan.compact else 2

    def bind(body, *first):
        return lambda *refs: body(*first, *refs)

    def swap(block, axis, first):
        return lax.ppermute(block, axis, swap_pairs(lax.axis_size(axis), first))

    rows_e, rows_o = pl.pallas_call(
        bind(stage_cut, plan),
        name="stage_cut",
        out_shape=[jax.ShapeDtypeStruct(plan.edge, BF16)] * 2,
        in_specs=[pl.BlockSpec(memory_space=pl.ANY)],
        out_specs=[VMEM, VMEM],
        scratch_shapes=[pltpu.SemaphoreType.DMA((2,))],
        compiler_params=pltpu.CompilerParams(vmem_limit_bytes=2**20),
    )(state)
    rows_e, rows_o, held_state = lax.optimization_barrier((rows_e, rows_o, state))
    near = [swap(held_state, "lev", side) for side in range(sides)]
    rows_e = swap(rows_e, "tile", 0)
    rows_o = swap(rows_o, "tile", 1)
    live = pltpu.SMEM(((plan.levels_n + 2) * plan.tall,), jnp.int32)
    own_cells = plan.own + (model,)
    qs, us, mid = call(
        bind(stage_own, plan),
        "stage_own",
        [(own_cells, BF16), (own_cells, BF16), ((plan.slots_n,) + plan.own[1:] + (2 * model,), BF16)],
        [ocean, depth, state, w_qkv, w_out, cotangent, *near],
        [live],
        cost=4 * 10**9,
    )
    rows_e, rows_o, qs = lax.optimization_barrier((rows_e, rows_o, qs))
    lev_in = []
    for side in range(sides):
        lev_in += [near[side], swap(rows_e, "lev", side), swap(rows_o, "lev", side)]
    rows = model // (tiles * levs)
    if levs == 2 and rows % 8 == 0:
        share = (tiles, rows, 4 * model)
        sums = [(share, F32), (share, BF16)]
    else:
        sums = [((model, 4 * model), F32)]
    keys_n = 3 * (PAIR + 2 * REACH) * width
    masks_n = 2 if plan.compact else plan.blocks_n
    masks = pltpu.VMEM((masks_n, keys_n, plan.queries_n), F32)
    weights = (HEADS // GROUP,) + plan.wide + (plan.blocks_n * plan.queries_n,)
    carried = [
        (plan.wide + (model,), BF16),
        (plan.wide + (2 * model,), BF16),
        (weights, BF16),
        (weights, BF16),
        (own_cells, BF16),
        (own_cells, BF16),
    ]
    held = call(
        bind(stage_inner, plan),
        "stage_inner",
        carried,
        [ocean, depth, state, rows_e, rows_o, qs, us, mid, w_qkv],
        [masks, live],
        mib=16,
        cost=8 * 10**9,
    )
    ins = [ocean, depth, state, qs, us, mid, w_qkv, cotangent, *lev_in, *held]
    _, _, _, _, attn, dq, dkv16, *sums = call(
        bind(stage_attend, plan, len(sums)),
        "stage_attend",
        carried + [(plan.wide + (2 * model,), BF16)] + sums,
        ins,
        [masks, live],
        mib=20,
        cost=16 * 10**9,
        aliases={len(ins) - len(held) + i: i for i in range(len(held))},
    )
    edge_kind = (plan.wide[1:] + (model,), BF16)
    out, own, part_e, part_o, *edges = call(
        bind(stage_out, plan),
        "stage_out",
        [(own_cells, BF16), (own_cells, F32), (plan.edge, F32), (plan.edge, F32)] + [edge_kind] * sides,
        [state, cotangent, attn, dq, dkv16, w_qkv, w_out],
        [pltpu.VMEM(plan.wide[1:] + (model,), F32)],
        cost=4 * 10**9,
    )
    edges = [swap(edge, "lev", side) for side, edge in enumerate(edges)]
    send_e, send_o = call(
        bind(stage_fold, plan),
        "stage_fold",
        [(plan.edge, BF16)] * 2,
        [part_e, part_o, *edges],
        [pltpu.VMEM(plan.edge, F32)],
    )

    if len(sums) == 2:
        x, parts = sums[0], [lax.ppermute(sums[1], "lev", swap_pairs(levs, 0))]
    else:
        x, parts = reduce_levels(sums[0], tiles, levs), []
    stride = 1
    for radix in digits(tiles):
        share = (x.shape[0] // radix,) + x.shape[1:]
        x, *pieces = call(
            bind(stage_split, len(parts), radix, stride),
            "stage_split",
            [(share, F32)] + [(share, BF16)] * (radix - 1),
            [x, *parts],
        )
        parts = [
            lax.ppermute(piece, "tile", xor_route(tiles, (k + 1) * stride))
            for k, piece in enumerate(pieces)
        ]
        if stride == 1:
            send_e, send_o, parts[2] = lax.optimization_barrier((send_e, send_o, parts[2]))
        stride *= radix
    back_e = swap(send_e, "tile", 0)
    back_o = swap(send_o, "tile", 1)
    d_state, d_qkv, d_out = call(
        bind(stage_last, plan, len(parts)),
        "stage_last",
        [(own_cells, BF16), ((rows, 3 * model), F32), ((rows, model), F32)],
        [own, back_e, back_o, x, *parts, *edges],
        [pltpu.VMEM(own_cells, F32)],
    )
    return (out, d_state, d_qkv, d_out)


def solution(mesh):
    placed = (P("lev", "tile", None, None), P(), P(), P("lev", "tile", None, None), P(), P())
    return jax.shard_map(
        local,
        mesh=mesh,
        in_specs=placed,
        out_specs=(
            P("lev", "tile", None, None),
            P("lev", "tile", None, None),
            P(("tile", "lev"), None),
            P(("tile", "lev"), None),
        ),
        check_vma=False,
    )
```

```python
import jax
import jax.numpy as jnp
from jax import lax
from jax.experimental import pallas as pl
from jax.experimental.pallas import tpu as pltpu
from jax.sharding import PartitionSpec as P

HEADS = 8
BROWS = 4
REACH = 3
GROUP = 4
PAIR = 2
LOW = -1e30
F32 = jnp.float32
BF16 = jnp.bfloat16
SMEM = pl.BlockSpec(memory_space=pltpu.SMEM)
VMEM = pl.BlockSpec(memory_space=pltpu.VMEM)


def dot(a, b, ca, cb):
    return lax.dot_general(a, b, (((ca,), (cb,)), ((), ())), preferred_element_type=F32)


def swap_pairs(count, first):
    route = []
    for i in range(first, count - 1, 2):
        route += [(i, i + 1), (i + 1, i)]
    return route


def call(body, name, outs, ins, scratch=(), mib=8, cost=10**6, aliases={}):
    return pl.pallas_call(
        body,
        name=name,
        out_shape=[jax.ShapeDtypeStruct(shape, kind) for shape, kind in outs],
        in_specs=[SMEM if x.dtype == jnp.int32 else VMEM for x in ins],
        out_specs=[VMEM] * len(outs),
        scratch_shapes=list(scratch),
        compiler_params=pltpu.CompilerParams(vmem_limit_bytes=mib * 2**20),
        input_output_aliases=aliases,
        cost_estimate=pl.CostEstimate(flops=cost, bytes_accessed=2**20, transcendentals=0),
    )(*ins)


class Plan:
    def __init__(self, shape, tiles, levs):
        self.levels_n, self.height, self.width, self.model = shape
        self.tiles, self.levs = tiles, levs
        self.tall = self.height + 2 * REACH
        self.compact = levs == 2 and self.levels_n == 2 and self.height == 2 * PAIR
        self.blocks_n = self.levels_n * self.height // PAIR
        self.lanes_n = GROUP * self.model // HEADS
        self.queries_n = GROUP * PAIR * self.width
        self.slots_n = self.levels_n + 2 - self.compact
        self.own = (self.levels_n, self.height, self.width)
        self.wide = (self.slots_n, self.tall, self.width)
        self.edge = (self.levels_n, REACH, self.width, self.model)

    def places(self):
        tile_odd = lax.rem(lax.axis_index("tile"), 2)
        lev_odd = lax.rem(lax.axis_index("lev"), 2)
        end = self.height + REACH
        self.even = tile_odd == 0
        self.at_e = jnp.where(tile_odd == 0, end, 0)
        self.at_o = jnp.where(tile_odd == 0, 0, end)
        self.off = 1 - lev_odd if self.compact else 0
        last = self.levels_n + 1
        self.slot_e = jnp.where(lev_odd == 0, last, 0) - self.off
        self.slot_o = jnp.where(lev_odd == 0, 0, last)
        self.first = 1 - self.off
        self.edge_e = jnp.where(lev_odd == 0, self.levels_n - 1, 0)
        self.edge_o = jnp.where(lev_odd == 0, 0, self.levels_n - 1)
        if self.compact:
            far = [(self.edge_o, r0, 2, self.first, 1) for r0 in (0, PAIR)]
            near = [(self.edge_e, r0, 3, 0, self.off) for r0 in (0, PAIR)]
            self.blocks = [far[0], near[0], near[1], far[1]]
        else:
            rows = range(0, self.height, PAIR)
            self.blocks = [(l, r0, 3, l, l) for l in range(self.levels_n) for r0 in rows]

    def liveness(self, ocean, depth, live):
        tile = lax.axis_index("tile")
        lev = lax.axis_index("lev")
        total_rows = self.height * self.tiles
        total_levels = self.levels_n * self.levs
        for r in range(self.tall):
            row = tile * self.height - REACH + r
            block_at = lax.div(jnp.clip(row, 0, total_rows - 1), BROWS)
            good = (row >= 0) & (row < total_rows) & (ocean[block_at] == 1)
            deep = depth[block_at]
            for l in range(self.levels_n + 2):
                at = lev * self.levels_n - 1 + l
                ok = good & (at >= 0) & (at < total_levels) & (at < deep)
                live[l * self.tall + r] = ok.astype(jnp.int32)

    def alive(self, live, level, row):
        return live[level * self.tall + row]


def stage_cut(plan, state, rows_e, rows_o, *refs):
    near, sems = refs[:-1], refs[-1]
    top = plan.height - REACH
    plan.places()
    at_e, at_o = jnp.where(plan.even, top, 0), jnp.where(plan.even, 0, top)
    cuts = [(state.at[:, pl.ds(at_e, REACH)], rows_e), (state.at[:, pl.ds(at_o, REACH)], rows_o)]
    cuts += [(state.at[level], edge) for level, edge in zip((plan.edge_e, plan.edge_o), near)]
    copies = [pltpu.make_async_copy(a, b, sems.at[i]) for i, (a, b) in enumerate(cuts)]
    for copy in copies:
        copy.start()
    for copy in copies:
        copy.wait()


def stage_own(plan, ocean, depth, state, w_qkv, w_out, cot, *refs):
    near, (qs, us, mid, live) = refs[:-4], refs[-4:]
    height, width, model = plan.own[1:] + (plan.model,)
    cells = height * width
    head = model // HEADS
    plan.places()
    plan.liveness(ocean, depth, live)

    def pairs(x):
        y = dot(x.reshape(cells, model), w_qkv[:, model:], 1, 0).astype(BF16)
        return y.reshape(height, width, 2 * model)

    for l in range(plan.levels_n):
        mid[plan.first + l] = pairs(state[l])
        flat = state[l].reshape(cells, model)
        q = dot(flat, w_qkv[:, :model], 1, 0).astype(BF16) * jnp.asarray(head**-0.5, BF16)
        qs[l] = q.reshape(height, width, model)
        u = dot(cot[l].reshape(cells, model), w_out[...], 1, 1).astype(BF16)
        u = u.reshape(height, width, model)
        for r in range(height):
            us[l, r] = u[r] * plan.alive(live, l + 1, REACH + r).astype(F32).astype(BF16)
    mid[plan.slot_e] = pairs(near[0][...])
    if not plan.compact:
        mid[plan.slot_o] = pairs(near[1][...])


def spread(plan, x):
    lane_head = lax.broadcasted_iota(jnp.int32, x.shape, 1) // (plan.model // HEADS)
    return jnp.concatenate(
        [jnp.where(lane_head == h, x, jnp.zeros_like(x)) for h in range(GROUP)], axis=0
    )


def group_lanes(plan, g):
    lanes = slice(g * plan.lanes_n, (g + 1) * plan.lanes_n)
    return lanes, slice(plan.model + lanes.start, plan.model + lanes.stop)


def spread_block(plan, x, block, lanes):
    l, r0 = block[:2]
    return spread(plan, x[l, r0 : r0 + PAIR, :, lanes].reshape(PAIR * plan.width, plan.lanes_n))


def attention(plan, numbers, live, qs, us, kv, bias, prob, grad, attn, dq):
    width, lanes_n, queries_n = plan.width, plan.lanes_n, plan.queries_n
    span = PAIR + 2 * REACH
    block_n = PAIR * width
    head = plan.model // HEADS
    lane_head = lax.broadcasted_iota(jnp.int32, (block_n, lanes_n), 1) // head
    query = lax.broadcasted_iota(jnp.int32, (width, queries_n), 1) % block_n
    query_row = query // width
    query_col = query % width
    key_col = lax.broadcasted_iota(jnp.int32, (width, queries_n), 0)
    near_col = jnp.abs(key_col - query_col) <= REACH

    def gather(x):
        total = jnp.where(lane_head == 0, x[:block_n], 0.0)
        for h in range(1, GROUP):
            total = jnp.where(lane_head == h, x[h * block_n : (h + 1) * block_n], total)
        return total

    def scores(slot, number, g):
        block = plan.blocks[number]
        l, r0, depth_n, base, _ = block
        keys_n = depth_n * span * width
        lanes, lanes_v = group_lanes(plan, g)
        q = spread_block(plan, qs, block, lanes)
        u = spread_block(plan, us, block, lanes)
        k = kv[pl.ds(base, depth_n), r0 : r0 + span, :, lanes].reshape(keys_n, lanes_n)
        v = kv[pl.ds(base, depth_n), r0 : r0 + span, :, lanes_v].reshape(keys_n, lanes_n)
        return k, v, dot(k, q, 1, 1) + bias[slot, :keys_n], dot(v, u, 1, 1)

    def weigh(s, dp):
        e = jnp.exp(s - jnp.max(s, axis=0, keepdims=True))
        inv = 1.0 / jnp.sum(e, axis=0, keepdims=True)
        delta = jnp.sum(e * dp, axis=0, keepdims=True) * inv
        p = e * inv
        return p.astype(BF16), (p * (dp - delta)).astype(BF16)

    def give(number, g, p16, ds16, k, v):
        l, r0, depth_n, base, _ = plan.blocks[number]
        lanes = group_lanes(plan, g)[0]
        at = slice(number * queries_n, (number + 1) * queries_n)
        tiled = (depth_n, span, width, queries_n)
        prob[g, pl.ds(base, depth_n), r0 : r0 + span, :, at] = p16.reshape(tiled)
        grad[g, pl.ds(base, depth_n), r0 : r0 + span, :, at] = ds16.reshape(tiled)
        a = gather(dot(p16, v, 0, 0))
        for r in range(PAIR):
            alive = plan.alive(live, l + 1, REACH + r0 + r).astype(F32)
            attn[l, r0 + r, :, lanes] = (a[r * width : (r + 1) * width] * alive).astype(BF16)
        b = gather(dot(ds16, k, 0, 0)) * (head**-0.5)
        dq[l, r0 : r0 + PAIR, :, lanes] = b.astype(BF16).reshape(PAIR, width, lanes_n)

    def mask(slot, number):
        _, r0, depth_n, _, base_level = plan.blocks[number]
        for dl in range(depth_n):
            for kr in range(span):
                alive = plan.alive(live, base_level + dl, r0 + kr) == 1
                near = near_col & (jnp.abs(query_row + REACH - kr) <= REACH)
                at = (dl * span + kr) * width
                bias[slot, at : at + width] = jnp.where(near & alive, 0.0, LOW)

    jobs = []
    for i, number in enumerate(numbers):
        mask(i, number)
        jobs += [(i, number, g) for g in range(HEADS // GROUP)]
    ready = [scores(*jobs[0])]
    for i, job in enumerate(jobs):
        if i + 1 < len(jobs):
            ready.append(scores(*jobs[i + 1]))
        k, v, s, dp = ready[i]
        give(*job[1:], *weigh(s, dp), k, v)


def sum_keys(plan, qs, us, prob, grad, dkv16):
    n = plan.queries_n
    if plan.compact:
        own, edge = pl.ds(plan.first, plan.levels_n), pl.ds(plan.slot_e, 1)
        end = plan.tall
        parts = [(own, plan.levels_n, 0, PAIR, 0, 2), (own, plan.levels_n, PAIR, end - PAIR, 0, 4)]
        parts += [(own, plan.levels_n, end - PAIR, end, 2, 4), (edge, 1, 0, PAIR, 1, 2)]
        parts += [(edge, 1, PAIR, end - PAIR, 1, 3), (edge, 1, end - PAIR, end, 2, 3)]
    else:
        parts = [(pl.ds(i, 1), 1, 0, plan.tall, 0, plan.blocks_n) for i in range(plan.slots_n)]
    for g in range(HEADS // GROUP):
        lanes, lanes_v = group_lanes(plan, g)
        for source, weights, at in ((qs, grad, lanes), (us, prob, lanes_v)):
            x = [spread_block(plan, source, block, lanes) for block in plan.blocks]
            x = jnp.concatenate(x, axis=0)
            for slots, slots_n, low, high, k0, k1 in parts:
                w = weights[g, slots, low:high, :, k0 * n : k1 * n]
                w = w.reshape(slots_n * (high - low) * plan.width, (k1 - k0) * n)
                y = dot(w, x[k0 * n : k1 * n], 1, 0).astype(BF16)
                dkv16[slots, low:high, :, at] = y.reshape(slots_n, high - low, plan.width, plan.lanes_n)


def project(plan, slot, ext, mid, w_qkv, kv):
    height, width = plan.own[1:]
    model = plan.model
    edge = REACH * width
    cells = [ext[slot, :REACH].reshape(edge, model), ext[slot, height + REACH :].reshape(edge, model)]
    pairs = dot(jnp.concatenate(cells, axis=0), w_qkv[:, model:], 1, 0).astype(BF16)
    kv[slot, :REACH] = pairs[:edge].reshape(REACH, width, 2 * model)
    kv[slot, height + REACH :] = pairs[edge:].reshape(REACH, width, 2 * model)
    kv[slot, REACH : height + REACH] = mid[slot]


def place_rows(plan, rows, at, w_qkv, ext, kv):
    slots = pl.ds(plan.first, plan.levels_n)
    ext[slots, pl.ds(at, REACH)] = rows[...]
    flat = rows[...].reshape(plan.levels_n * REACH * plan.width, plan.model)
    pairs = dot(flat, w_qkv[:, plan.model :], 1, 0).astype(BF16)
    kv[slots, pl.ds(at, REACH)] = pairs.reshape(plan.levels_n, REACH, plan.width, 2 * plan.model)


def stage_side(plan, state, rows_e, mid, w_qkv, ext, kv):
    plan.places()
    slots = pl.ds(plan.first, plan.levels_n)
    ext[slots, REACH : plan.height + REACH] = state[...]
    kv[slots, REACH : plan.height + REACH] = mid[slots]
    place_rows(plan, rows_e, plan.at_e, w_qkv, ext, kv)


def stage_inner(plan, ocean, depth, rows_o, qs, us, w_qkv, *refs):
    ext, kv, prob, grad, attn, dq, bias, live = refs[2:]
    plan.places()
    plan.liveness(ocean, depth, live)
    place_rows(plan, rows_o, plan.at_o, w_qkv, ext, kv)
    if plan.compact:
        attention(plan, (0, 3), live, qs, us, kv, bias, prob, grad, attn, dq)


def stage_attend(plan, sums_n, ocean, depth, state, qs, us, mid, w_qkv, cot, *refs):
    sides = 1 if plan.compact else 2
    lev_in, refs = refs[: 3 * sides], refs[3 * sides + 6 :]
    ext, kv, prob, grad, attn, dq, dkv16 = refs[:7]
    sums, (bias, live) = refs[7 : 7 + sums_n], refs[7 + sums_n :]
    levels_n, height, width = plan.own
    model, tall = plan.model, plan.tall
    plan.places()
    plan.liveness(ocean, depth, live)
    for side, (slot, level) in enumerate(((plan.slot_e, plan.edge_o), (plan.slot_o, plan.edge_e))):
        if side < sides:
            near, far_e, far_o = lev_in[3 * side : 3 * side + 3]
            ext[slot, REACH : height + REACH] = near[...]
            ext[slot, pl.ds(plan.at_e, REACH)] = far_e[level]
            ext[slot, pl.ds(plan.at_o, REACH)] = far_o[level]
            project(plan, slot, ext, mid, w_qkv, kv)
    if plan.compact:
        numbers = (1, 2)
    else:
        numbers = range(plan.blocks_n)
        prob[...] = jnp.zeros(prob.shape, BF16)
        grad[...] = jnp.zeros(grad.shape, BF16)
    attention(plan, numbers, live, qs, us, kv, bias, prob, grad, attn, dq)
    sum_keys(plan, qs, us, prob, grad, dkv16)
    cells = levels_n * height * width
    wide = plan.slots_n * tall * width

    def emit(at, x):
        n = x.shape[1]
        if sums_n == 1:
            sums[0][:, at : at + n] = x
            return
        keep, send = sums
        rows = model // (plan.tiles * plan.levs)
        x = x.reshape(plan.tiles, plan.levs, rows, n)
        mine = lax.axis_index("lev") == 0
        keep[:, :, at : at + n] = jnp.where(mine, x[:, 0], x[:, 1])
        send[:, :, at : at + n] = jnp.where(mine, x[:, 1], x[:, 0]).astype(BF16)

    emit(0, dot(state[...].reshape(cells, model), dq[...].reshape(cells, model), 0, 0))
    emit(3 * model, dot(attn[...].reshape(cells, model), cot[...].reshape(cells, model), 0, 0))
    for j in range(2):
        part = dkv16[:, :, :, j * model : (j + 1) * model].reshape(wide, model)
        emit((j + 1) * model, dot(ext[...].reshape(wide, model), part, 0, 0))


def stage_out(plan, dkv16, w_qkv, inner, rows_e, rows_o, *refs):
    edges, tmp = refs[:-1], refs[-1]
    levels_n, height, width = plan.own
    model, tall = plan.model, plan.tall
    plan.places()

    def back(slot):
        x = dot(dkv16[slot].reshape(tall * width, 2 * model), w_qkv[:, model:], 1, 1)
        return x.reshape(tall, width, model)

    for edge, slot in zip(edges, (plan.slot_e, plan.slot_o)):
        edge[...] = back(slot).astype(BF16)
    for l in range(levels_n):
        tmp[...] = back(plan.first + l)
        rows_e[l] = tmp[pl.ds(plan.at_e, REACH)]
        rows_o[l] = tmp[pl.ds(plan.at_o, REACH)]
        inner[l] = tmp[REACH : REACH + height]


def stage_fold(plan, rows_e, rows_o, inner, state, cot, attn, dq, w_qkv, w_out, *refs):
    edges, (send_e, send_o, out, own, acc) = refs[:-5], refs[-5:]
    levels_n, height, width = plan.own
    model = plan.model
    cells = height * width
    plan.places()
    for rows, at, send in ((rows_e, plan.at_e, send_e), (rows_o, plan.at_o, send_o)):
        acc[...] = rows[...]
        for edge, level in zip(edges, (plan.edge_e, plan.edge_o)):
            acc[level] += edge[pl.ds(at, REACH)].astype(F32)
        send[...] = acc[...].astype(BF16)
    for l in range(levels_n):
        x = cot[l].reshape(cells, model).astype(F32)
        x = x + dot(dq[l].reshape(cells, model), w_qkv[:, :model], 1, 1)
        own[l] = x.reshape(height, width, model) + inner[l]
        x = state[l].reshape(cells, model).astype(F32)
        x = x + dot(attn[l].reshape(cells, model), w_out[...], 1, 0)
        out[l] = x.astype(BF16).reshape(height, width, model)


def stage_last(plan, parts_n, own, back_e, back_o, x, *refs):
    parts, edges, (d_state, d_qkv, d_out, acc) = refs[:parts_n], refs[parts_n:-4], refs[-4:]
    plan.places()
    height = plan.height
    acc[...] = own[...]
    for edge, level in zip(edges, (plan.edge_e, plan.edge_o)):
        acc[level] += edge[REACH : REACH + height].astype(F32)
    top = height - REACH
    acc[:, pl.ds(jnp.where(plan.even, top, 0), REACH)] += back_e[...].astype(F32)
    acc[:, pl.ds(jnp.where(plan.even, 0, top), REACH)] += back_o[...].astype(F32)
    d_state[...] = acc[...].astype(BF16)
    y = x[0]
    for part in parts:
        y = y + part[0].astype(F32)
    cut = d_qkv.shape[1]
    d_qkv[...] = y[:, :cut]
    d_out[...] = y[:, cut:]


def stage_split(parts_n, radix, stride, x, *refs):
    parts, (own, *pieces) = refs[:parts_n], refs[parts_n:]
    digit = lax.rem(lax.div(lax.axis_index("tile"), stride), radix)
    for h in range(x.shape[0] // radix):
        for k in range(radix):
            at = h * radix + jnp.bitwise_xor(digit, k)
            y = x[at]
            for part in parts:
                y = y + part[at].astype(F32)
            if k == 0:
                own[h] = y
            else:
                pieces[k - 1][h] = y.astype(BF16)


def digits(count):
    sizes = []
    while count > 1:
        radix = 4 if count % 4 == 0 else 2
        sizes.append(radix)
        count //= radix
    return sizes


def xor_route(count, step):
    return [(i, i ^ step) for i in range(count)]


def reduce_levels(x, tiles, levs):
    rows, cols = x.shape
    x = x.reshape([tiles] + digits(levs)[::-1] + [rows // (tiles * levs), cols])
    stride = 1
    for radix in digits(levs):
        dim = x.ndim - 3
        digit = lax.rem(lax.div(lax.axis_index("lev"), stride), radix)
        total = lax.dynamic_index_in_dim(x, digit, dim, keepdims=False)
        for k in range(1, radix):
            piece = lax.dynamic_index_in_dim(x, jnp.bitwise_xor(digit, k), dim, keepdims=False)
            piece = lax.ppermute(piece.astype(BF16), "lev", xor_route(levs, k * stride))
            total = total + piece.astype(F32)
        x = total
        stride *= radix
    return x


def local(state, w_qkv, w_out, cotangent, ocean, depth):
    tiles, levs = lax.axis_size("tile"), lax.axis_size("lev")
    plan = Plan(state.shape, tiles, levs)
    height, width, model = plan.height, plan.width, plan.model
    sides = 1 if plan.compact else 2

    def bind(body, *first):
        return lambda *refs: body(*first, *refs)

    def swap(block, axis, first):
        return lax.ppermute(block, axis, swap_pairs(lax.axis_size(axis), first))

    rows_e, rows_o, *near = pl.pallas_call(
        bind(stage_cut, plan),
        name="stage_cut",
        out_shape=[jax.ShapeDtypeStruct(plan.edge, BF16)] * 2
        + [jax.ShapeDtypeStruct(plan.own[1:] + (model,), BF16)] * sides,
        in_specs=[pl.BlockSpec(memory_space=pl.ANY)],
        out_specs=[VMEM] * (2 + sides),
        scratch_shapes=[pltpu.SemaphoreType.DMA((2 + sides,))],
        compiler_params=pltpu.CompilerParams(vmem_limit_bytes=2**20),
        cost_estimate=pl.CostEstimate(flops=20 * 10**9, bytes_accessed=2**20, transcendentals=0),
    )(state)
    near = [swap(edge, "lev", side) for side, edge in enumerate(near)]
    rows_e = swap(rows_e, "tile", 0)
    rows_o = swap(rows_o, "tile", 1)
    live = pltpu.SMEM(((plan.levels_n + 2) * plan.tall,), jnp.int32)
    own_cells = plan.own + (model,)
    qs, us, mid = call(
        bind(stage_own, plan),
        "stage_own",
        [(own_cells, BF16), (own_cells, BF16), ((plan.slots_n,) + plan.own[1:] + (2 * model,), BF16)],
        [ocean, depth, state, w_qkv, w_out, cotangent, *near],
        [live],
        cost=4 * 10**9,
    )
    rows_e, qs = lax.optimization_barrier((rows_e, qs))
    rows = model // (tiles * levs)
    if levs == 2 and rows % 8 == 0:
        share = (tiles, rows, 4 * model)
        sums = [(share, F32), (share, BF16)]
    else:
        sums = [((model, 4 * model), F32)]
    keys_n = 3 * (PAIR + 2 * REACH) * width
    masks_n = 2 if plan.compact else plan.blocks_n
    masks = pltpu.VMEM((masks_n, keys_n, plan.queries_n), F32)
    weights = (HEADS // GROUP,) + plan.wide + (plan.blocks_n * plan.queries_n,)
    carried = [
        (plan.wide + (model,), BF16),
        (plan.wide + (2 * model,), BF16),
        (weights, BF16),
        (weights, BF16),
        (own_cells, BF16),
        (own_cells, BF16),
    ]
    side = call(
        bind(stage_side, plan),
        "stage_side",
        carried[:2],
        [state, rows_e, mid, w_qkv],
        cost=2 * 10**9,
    )
    rows_o, *side = lax.optimization_barrier((rows_o, *side))
    lev_in = []
    for n in range(sides):
        lev_in += [near[n], swap(rows_e, "lev", n), swap(rows_o, "lev", n)]
    held = call(
        bind(stage_inner, plan),
        "stage_inner",
        carried,
        [ocean, depth, rows_o, qs, us, w_qkv, *side],
        [masks, live],
        mib=16,
        cost=8 * 10**9,
        aliases={6: 0, 7: 1},
    )
    ins = [ocean, depth, state, qs, us, mid, w_qkv, cotangent, *lev_in, *held]
    _, _, _, _, attn, dq, dkv16, *sums = call(
        bind(stage_attend, plan, len(sums)),
        "stage_attend",
        carried + [(plan.wide + (2 * model,), BF16)] + sums,
        ins,
        [masks, live],
        mib=20,
        cost=16 * 10**9,
        aliases={len(ins) - len(held) + i: i for i in range(len(held))},
    )
    edge_kind = (plan.wide[1:] + (model,), BF16)
    inner, part_e, part_o, *edges = call(
        bind(stage_out, plan),
        "stage_out",
        [(own_cells, F32), (plan.edge, F32), (plan.edge, F32)] + [edge_kind] * sides,
        [dkv16, w_qkv],
        [pltpu.VMEM(plan.wide[1:] + (model,), F32)],
        cost=4 * 10**9,
    )
    edges = [swap(edge, "lev", side) for side, edge in enumerate(edges)]
    send_e, send_o, out, own = call(
        bind(stage_fold, plan),
        "stage_fold",
        [(plan.edge, BF16)] * 2 + [(own_cells, BF16), (own_cells, F32)],
        [part_e, part_o, inner, state, cotangent, attn, dq, w_qkv, w_out, *edges],
        [pltpu.VMEM(plan.edge, F32)],
    )

    if len(sums) == 2:
        x, parts = sums[0], [lax.ppermute(sums[1], "lev", swap_pairs(levs, 0))]
    else:
        x, parts = reduce_levels(sums[0], tiles, levs), []
    stride = 1
    for radix in digits(tiles):
        share = (x.shape[0] // radix,) + x.shape[1:]
        x, *pieces = call(
            bind(stage_split, len(parts), radix, stride),
            "stage_split",
            [(share, F32)] + [(share, BF16)] * (radix - 1),
            [x, *parts],
        )
        parts = [
            lax.ppermute(piece, "tile", xor_route(tiles, (k + 1) * stride))
            for k, piece in enumerate(pieces)
        ]
        if stride == 1:
            send_e, send_o, parts[2] = lax.optimization_barrier((send_e, send_o, parts[2]))
        stride *= radix
    back_e = swap(send_e, "tile", 0)
    back_o = swap(send_o, "tile", 1)
    d_state, d_qkv, d_out = call(
        bind(stage_last, plan, len(parts)),
        "stage_last",
        [(own_cells, BF16), ((rows, 3 * model), F32), ((rows, model), F32)],
        [own, back_e, back_o, x, *parts, *edges],
        [pltpu.VMEM(own_cells, F32)],
    )
    return (out, d_state, d_qkv, d_out)


def solution(mesh):
    placed = (P("lev", "tile", None, None), P(), P(), P("lev", "tile", None, None), P(), P())
    return jax.shard_map(
        local,
        mesh=mesh,
        in_specs=placed,
        out_specs=(
            P("lev", "tile", None, None),
            P("lev", "tile", None, None),
            P(("tile", "lev"), None),
            P(("tile", "lev"), None),
        ),
        check_vma=False,
    )
```

```python
import jax
import jax.numpy as jnp
from jax import lax
from jax.experimental import pallas as pl
from jax.experimental.pallas import tpu as pltpu
from jax.sharding import PartitionSpec as P

HEADS = 8
BROWS = 4
REACH = 3
GROUP = 4
PAIR = 2
LOW = -1e30
F32 = jnp.float32
BF16 = jnp.bfloat16
SMEM = pl.BlockSpec(memory_space=pltpu.SMEM)
VMEM = pl.BlockSpec(memory_space=pltpu.VMEM)


def dot(a, b, ca, cb):
    return lax.dot_general(a, b, (((ca,), (cb,)), ((), ())), preferred_element_type=F32)


def swap_pairs(count, first):
    route = []
    for i in range(first, count - 1, 2):
        route += [(i, i + 1), (i + 1, i)]
    return route


def call(body, name, outs, ins, scratch=(), mib=8, cost=10**6, aliases={}):
    return pl.pallas_call(
        body,
        name=name,
        out_shape=[jax.ShapeDtypeStruct(shape, kind) for shape, kind in outs],
        in_specs=[SMEM if x.dtype == jnp.int32 else VMEM for x in ins],
        out_specs=[VMEM] * len(outs),
        scratch_shapes=list(scratch),
        compiler_params=pltpu.CompilerParams(vmem_limit_bytes=mib * 2**20),
        input_output_aliases=aliases,
        cost_estimate=pl.CostEstimate(flops=cost, bytes_accessed=2**20, transcendentals=0),
    )(*ins)


class Plan:
    def __init__(self, shape, tiles, levs):
        self.levels_n, self.height, self.width, self.model = shape
        self.tiles, self.levs = tiles, levs
        self.tall = self.height + 2 * REACH
        self.compact = levs == 2 and self.levels_n == 2 and self.height == 2 * PAIR
        self.blocks_n = self.levels_n * self.height // PAIR
        self.lanes_n = GROUP * self.model // HEADS
        self.queries_n = GROUP * PAIR * self.width
        self.slots_n = self.levels_n + 2 - self.compact
        self.own = (self.levels_n, self.height, self.width)
        self.wide = (self.slots_n, self.tall, self.width)
        self.edge = (self.levels_n, REACH, self.width, self.model)

    def places(self):
        tile_odd = lax.rem(lax.axis_index("tile"), 2)
        lev_odd = lax.rem(lax.axis_index("lev"), 2)
        end = self.height + REACH
        self.even = tile_odd == 0
        self.at_e = jnp.where(tile_odd == 0, end, 0)
        self.at_o = jnp.where(tile_odd == 0, 0, end)
        self.off = 1 - lev_odd if self.compact else 0
        last = self.levels_n + 1
        self.slot_e = jnp.where(lev_odd == 0, last, 0) - self.off
        self.slot_o = jnp.where(lev_odd == 0, 0, last)
        self.first = 1 - self.off
        self.edge_e = jnp.where(lev_odd == 0, self.levels_n - 1, 0)
        self.edge_o = jnp.where(lev_odd == 0, 0, self.levels_n - 1)
        if self.compact:
            far = [(self.edge_o, r0, 2, self.first, 1) for r0 in (0, PAIR)]
            near = [(self.edge_e, r0, 3, 0, self.off) for r0 in (0, PAIR)]
            self.blocks = [far[0], near[0], near[1], far[1]]
        else:
            rows = range(0, self.height, PAIR)
            self.blocks = [(l, r0, 3, l, l) for l in range(self.levels_n) for r0 in rows]

    def liveness(self, ocean, depth, live):
        tile = lax.axis_index("tile")
        lev = lax.axis_index("lev")
        total_rows = self.height * self.tiles
        total_levels = self.levels_n * self.levs
        for r in range(self.tall):
            row = tile * self.height - REACH + r
            block_at = lax.div(jnp.clip(row, 0, total_rows - 1), BROWS)
            good = (row >= 0) & (row < total_rows) & (ocean[block_at] == 1)
            deep = depth[block_at]
            for l in range(self.levels_n + 2):
                at = lev * self.levels_n - 1 + l
                ok = good & (at >= 0) & (at < total_levels) & (at < deep)
                live[l * self.tall + r] = ok.astype(jnp.int32)

    def alive(self, live, level, row):
        return live[level * self.tall + row]


def stage_cut(plan, state, rows_e, rows_o, *refs):
    near, sems = refs[:-1], refs[-1]
    top = plan.height - REACH
    plan.places()
    at_e, at_o = jnp.where(plan.even, top, 0), jnp.where(plan.even, 0, top)
    cuts = [(state.at[:, pl.ds(at_e, REACH)], rows_e), (state.at[:, pl.ds(at_o, REACH)], rows_o)]
    cuts += [(state.at[level], edge) for level, edge in zip((plan.edge_e, plan.edge_o), near)]
    copies = [pltpu.make_async_copy(a, b, sems.at[i]) for i, (a, b) in enumerate(cuts)]
    for copy in copies:
        copy.start()
    for copy in copies:
        copy.wait()


def stage_own(plan, ocean, depth, state, w_qkv, w_out, cot, *refs):
    near, (qs, us, mid, live) = refs[:-4], refs[-4:]
    height, width, model = plan.own[1:] + (plan.model,)
    cells = height * width
    head = model // HEADS
    plan.places()
    plan.liveness(ocean, depth, live)

    def pairs(x):
        y = dot(x.reshape(cells, model), w_qkv[:, model:], 1, 0).astype(BF16)
        return y.reshape(height, width, 2 * model)

    for l in range(plan.levels_n):
        mid[plan.first + l] = pairs(state[l])
        flat = state[l].reshape(cells, model)
        q = dot(flat, w_qkv[:, :model], 1, 0).astype(BF16) * jnp.asarray(head**-0.5, BF16)
        qs[l] = q.reshape(height, width, model)
        u = dot(cot[l].reshape(cells, model), w_out[...], 1, 1).astype(BF16)
        u = u.reshape(height, width, model)
        for r in range(height):
            us[l, r] = u[r] * plan.alive(live, l + 1, REACH + r).astype(F32).astype(BF16)
    mid[plan.slot_e] = pairs(near[0][...])
    if not plan.compact:
        mid[plan.slot_o] = pairs(near[1][...])


def spread(plan, x):
    lane_head = lax.broadcasted_iota(jnp.int32, x.shape, 1) // (plan.model // HEADS)
    return jnp.concatenate(
        [jnp.where(lane_head == h, x, jnp.zeros_like(x)) for h in range(GROUP)], axis=0
    )


def group_lanes(plan, g):
    lanes = slice(g * plan.lanes_n, (g + 1) * plan.lanes_n)
    return lanes, slice(plan.model + lanes.start, plan.model + lanes.stop)


def spread_block(plan, x, block, lanes):
    l, r0 = block[:2]
    return spread(plan, x[l, r0 : r0 + PAIR, :, lanes].reshape(PAIR * plan.width, plan.lanes_n))


def attention(plan, numbers, live, qs, us, kv, bias, prob, grad, attn, dq):
    width, lanes_n, queries_n = plan.width, plan.lanes_n, plan.queries_n
    span = PAIR + 2 * REACH
    block_n = PAIR * width
    head = plan.model // HEADS
    lane_head = lax.broadcasted_iota(jnp.int32, (block_n, lanes_n), 1) // head
    query = lax.broadcasted_iota(jnp.int32, (width, queries_n), 1) % block_n
    query_row = query // width
    query_col = query % width
    key_col = lax.broadcasted_iota(jnp.int32, (width, queries_n), 0)
    near_col = jnp.abs(key_col - query_col) <= REACH

    def gather(x):
        total = jnp.where(lane_head == 0, x[:block_n], 0.0)
        for h in range(1, GROUP):
            total = jnp.where(lane_head == h, x[h * block_n : (h + 1) * block_n], total)
        return total

    def scores(slot, number, g):
        block = plan.blocks[number]
        l, r0, depth_n, base, _ = block
        keys_n = depth_n * span * width
        lanes, lanes_v = group_lanes(plan, g)
        q = spread_block(plan, qs, block, lanes)
        u = spread_block(plan, us, block, lanes)
        k = kv[pl.ds(base, depth_n), r0 : r0 + span, :, lanes].reshape(keys_n, lanes_n)
        v = kv[pl.ds(base, depth_n), r0 : r0 + span, :, lanes_v].reshape(keys_n, lanes_n)
        return k, v, dot(k, q, 1, 1) + bias[slot, :keys_n], dot(v, u, 1, 1)

    def weigh(s, dp):
        e = jnp.exp(s - jnp.max(s, axis=0, keepdims=True))
        inv = 1.0 / jnp.sum(e, axis=0, keepdims=True)
        delta = jnp.sum(e * dp, axis=0, keepdims=True) * inv
        p = e * inv
        return p.astype(BF16), (p * (dp - delta)).astype(BF16)

    def give(number, g, p16, ds16, k, v):
        l, r0, depth_n, base, _ = plan.blocks[number]
        lanes = group_lanes(plan, g)[0]
        at = slice(number * queries_n, (number + 1) * queries_n)
        tiled = (depth_n, span, width, queries_n)
        prob[g, pl.ds(base, depth_n), r0 : r0 + span, :, at] = p16.reshape(tiled)
        grad[g, pl.ds(base, depth_n), r0 : r0 + span, :, at] = ds16.reshape(tiled)
        a = gather(dot(p16, v, 0, 0))
        for r in range(PAIR):
            alive = plan.alive(live, l + 1, REACH + r0 + r).astype(F32)
            attn[l, r0 + r, :, lanes] = (a[r * width : (r + 1) * width] * alive).astype(BF16)
        b = gather(dot(ds16, k, 0, 0)) * (head**-0.5)
        dq[l, r0 : r0 + PAIR, :, lanes] = b.astype(BF16).reshape(PAIR, width, lanes_n)

    def mask(slot, number):
        _, r0, depth_n, _, base_level = plan.blocks[number]
        for dl in range(depth_n):
            for kr in range(span):
                alive = plan.alive(live, base_level + dl, r0 + kr) == 1
                near = near_col & (jnp.abs(query_row + REACH - kr) <= REACH)
                at = (dl * span + kr) * width
                bias[slot, at : at + width] = jnp.where(near & alive, 0.0, LOW)

    jobs = []
    for i, number in enumerate(numbers):
        mask(i, number)
        jobs += [(i, number, g) for g in range(HEADS // GROUP)]
    ready = [scores(*jobs[0])]
    for i, job in enumerate(jobs):
        if i + 1 < len(jobs):
            ready.append(scores(*jobs[i + 1]))
        k, v, s, dp = ready[i]
        give(*job[1:], *weigh(s, dp), k, v)


def sum_keys(plan, qs, us, prob, grad, dkv16):
    n = plan.queries_n
    if plan.compact:
        own, edge = pl.ds(plan.first, plan.levels_n), pl.ds(plan.slot_e, 1)
        end = plan.tall
        parts = [(own, plan.levels_n, 0, PAIR, 0, 2), (own, plan.levels_n, PAIR, end - PAIR, 0, 4)]
        parts += [(own, plan.levels_n, end - PAIR, end, 2, 4), (edge, 1, 0, PAIR, 1, 2)]
        parts += [(edge, 1, PAIR, end - PAIR, 1, 3), (edge, 1, end - PAIR, end, 2, 3)]
    else:
        parts = [(pl.ds(i, 1), 1, 0, plan.tall, 0, plan.blocks_n) for i in range(plan.slots_n)]
    for g in range(HEADS // GROUP):
        lanes, lanes_v = group_lanes(plan, g)
        for source, weights, at in ((qs, grad, lanes), (us, prob, lanes_v)):
            x = [spread_block(plan, source, block, lanes) for block in plan.blocks]
            x = jnp.concatenate(x, axis=0)
            for slots, slots_n, low, high, k0, k1 in parts:
                w = weights[g, slots, low:high, :, k0 * n : k1 * n]
                w = w.reshape(slots_n * (high - low) * plan.width, (k1 - k0) * n)
                y = dot(w, x[k0 * n : k1 * n], 1, 0).astype(BF16)
                dkv16[slots, low:high, :, at] = y.reshape(slots_n, high - low, plan.width, plan.lanes_n)


def project(plan, slot, ext, mid, w_qkv, kv):
    height, width = plan.own[1:]
    model = plan.model
    edge = REACH * width
    cells = [ext[slot, :REACH].reshape(edge, model), ext[slot, height + REACH :].reshape(edge, model)]
    pairs = dot(jnp.concatenate(cells, axis=0), w_qkv[:, model:], 1, 0).astype(BF16)
    kv[slot, :REACH] = pairs[:edge].reshape(REACH, width, 2 * model)
    kv[slot, height + REACH :] = pairs[edge:].reshape(REACH, width, 2 * model)
    kv[slot, REACH : height + REACH] = mid[slot]


def place_rows(plan, rows, at, w_qkv, ext, kv):
    slots = pl.ds(plan.first, plan.levels_n)
    ext[slots, pl.ds(at, REACH)] = rows[...]
    flat = rows[...].reshape(plan.levels_n * REACH * plan.width, plan.model)
    pairs = dot(flat, w_qkv[:, plan.model :], 1, 0).astype(BF16)
    kv[slots, pl.ds(at, REACH)] = pairs.reshape(plan.levels_n, REACH, plan.width, 2 * plan.model)


def stage_side(plan, state, rows_e, mid, w_qkv, ext, kv):
    plan.places()
    slots = pl.ds(plan.first, plan.levels_n)
    ext[slots, REACH : plan.height + REACH] = state[...]
    kv[slots, REACH : plan.height + REACH] = mid[slots]
    place_rows(plan, rows_e, plan.at_e, w_qkv, ext, kv)


def stage_inner(plan, ocean, depth, rows_o, qs, us, w_qkv, *refs):
    ext, kv, prob, grad, attn, dq, bias, live = refs[2:]
    plan.places()
    plan.liveness(ocean, depth, live)
    place_rows(plan, rows_o, plan.at_o, w_qkv, ext, kv)
    if plan.compact:
        attention(plan, (0, 3), live, qs, us, kv, bias, prob, grad, attn, dq)


def stage_attend(plan, sums_n, ocean, depth, state, qs, us, mid, w_qkv, cot, *refs):
    sides = 1 if plan.compact else 2
    lev_in, refs = refs[: 3 * sides], refs[3 * sides + 6 :]
    ext, kv, prob, grad, attn, dq, dkv16 = refs[:7]
    sums, (bias, live) = refs[7 : 7 + sums_n], refs[7 + sums_n :]
    levels_n, height, width = plan.own
    model, tall = plan.model, plan.tall
    plan.places()
    plan.liveness(ocean, depth, live)
    for side, (slot, level) in enumerate(((plan.slot_e, plan.edge_o), (plan.slot_o, plan.edge_e))):
        if side < sides:
            near, far_e, far_o = lev_in[3 * side : 3 * side + 3]
            ext[slot, REACH : height + REACH] = near[...]
            ext[slot, pl.ds(plan.at_e, REACH)] = far_e[level]
            ext[slot, pl.ds(plan.at_o, REACH)] = far_o[level]
            project(plan, slot, ext, mid, w_qkv, kv)
    if plan.compact:
        numbers = (1, 2)
    else:
        numbers = range(plan.blocks_n)
        prob[...] = jnp.zeros(prob.shape, BF16)
        grad[...] = jnp.zeros(grad.shape, BF16)
    attention(plan, numbers, live, qs, us, kv, bias, prob, grad, attn, dq)
    sum_keys(plan, qs, us, prob, grad, dkv16)
    cells = levels_n * height * width
    wide = plan.slots_n * tall * width

    def emit(at, x):
        n = x.shape[1]
        if sums_n == 1:
            sums[0][:, at : at + n] = x
            return
        keep, send = sums
        rows = model // (plan.tiles * plan.levs)
        x = x.reshape(plan.tiles, plan.levs, rows, n)
        mine = lax.axis_index("lev") == 0
        keep[:, :, at : at + n] = jnp.where(mine, x[:, 0], x[:, 1])
        send[:, :, at : at + n] = jnp.where(mine, x[:, 1], x[:, 0]).astype(BF16)

    emit(0, dot(state[...].reshape(cells, model), dq[...].reshape(cells, model), 0, 0))
    emit(3 * model, dot(attn[...].reshape(cells, model), cot[...].reshape(cells, model), 0, 0))
    for j in range(2):
        part = dkv16[:, :, :, j * model : (j + 1) * model].reshape(wide, model)
        emit((j + 1) * model, dot(ext[...].reshape(wide, model), part, 0, 0))


def stage_out(plan, dkv16, w_qkv, inner, rows_e, rows_o, *refs):
    edges, tmp = refs[:-1], refs[-1]
    levels_n, height, width = plan.own
    model, tall = plan.model, plan.tall
    plan.places()

    def back(slot):
        x = dot(dkv16[slot].reshape(tall * width, 2 * model), w_qkv[:, model:], 1, 1)
        return x.reshape(tall, width, model)

    for edge, slot in zip(edges, (plan.slot_e, plan.slot_o)):
        edge[...] = back(slot).astype(BF16)
    for l in range(levels_n):
        tmp[...] = back(plan.first + l)
        rows_e[l] = tmp[pl.ds(plan.at_e, REACH)]
        rows_o[l] = tmp[pl.ds(plan.at_o, REACH)]
        inner[l] = tmp[REACH : REACH + height]


def stage_fold(plan, rows_e, rows_o, inner, state, cot, attn, dq, w_qkv, w_out, *refs):
    edges, (send_e, send_o, out, own, acc) = refs[:-5], refs[-5:]
    levels_n, height, width = plan.own
    model = plan.model
    cells = height * width
    plan.places()
    for rows, at, send in ((rows_e, plan.at_e, send_e), (rows_o, plan.at_o, send_o)):
        acc[...] = rows[...]
        for edge, level in zip(edges, (plan.edge_e, plan.edge_o)):
            acc[level] += edge[pl.ds(at, REACH)].astype(F32)
        send[...] = acc[...].astype(BF16)
    for l in range(levels_n):
        x = cot[l].reshape(cells, model).astype(F32)
        x = x + dot(dq[l].reshape(cells, model), w_qkv[:, :model], 1, 1)
        own[l] = x.reshape(height, width, model) + inner[l]
        x = state[l].reshape(cells, model).astype(F32)
        x = x + dot(attn[l].reshape(cells, model), w_out[...], 1, 0)
        out[l] = x.astype(BF16).reshape(height, width, model)


def stage_last(plan, own, back_e, back_o, *refs):
    edges, (d_state, acc) = refs[:-2], refs[-2:]
    plan.places()
    height = plan.height
    acc[...] = own[...]
    for edge, level in zip(edges, (plan.edge_e, plan.edge_o)):
        acc[level] += edge[REACH : REACH + height].astype(F32)
    top = height - REACH
    acc[:, pl.ds(jnp.where(plan.even, top, 0), REACH)] += back_e[...].astype(F32)
    acc[:, pl.ds(jnp.where(plan.even, 0, top), REACH)] += back_o[...].astype(F32)
    d_state[...] = acc[...].astype(BF16)


def stage_sum(x, *refs):
    parts, (d_qkv, d_out) = refs[:-2], refs[-2:]
    y = x[0]
    for part in parts:
        y = y + part[0].astype(F32)
    cut = d_qkv.shape[1]
    d_qkv[...] = y[:, :cut]
    d_out[...] = y[:, cut:]


def stage_split(parts_n, radix, stride, x, *refs):
    parts, (own, *pieces) = refs[:parts_n], refs[parts_n:]
    digit = lax.rem(lax.div(lax.axis_index("tile"), stride), radix)
    for h in range(x.shape[0] // radix):
        for k in range(radix):
            at = h * radix + jnp.bitwise_xor(digit, k)
            y = x[at]
            for part in parts:
                y = y + part[at].astype(F32)
            if k == 0:
                own[h] = y
            else:
                pieces[k - 1][h] = y.astype(BF16)


def digits(count):
    sizes = []
    while count > 1:
        radix = 4 if count % 4 == 0 else 2
        sizes.append(radix)
        count //= radix
    return sizes


def xor_route(count, step):
    return [(i, i ^ step) for i in range(count)]


def reduce_levels(x, tiles, levs):
    rows, cols = x.shape
    x = x.reshape([tiles] + digits(levs)[::-1] + [rows // (tiles * levs), cols])
    stride = 1
    for radix in digits(levs):
        dim = x.ndim - 3
        digit = lax.rem(lax.div(lax.axis_index("lev"), stride), radix)
        total = lax.dynamic_index_in_dim(x, digit, dim, keepdims=False)
        for k in range(1, radix):
            piece = lax.dynamic_index_in_dim(x, jnp.bitwise_xor(digit, k), dim, keepdims=False)
            piece = lax.ppermute(piece.astype(BF16), "lev", xor_route(levs, k * stride))
            total = total + piece.astype(F32)
        x = total
        stride *= radix
    return x


def local(state, w_qkv, w_out, cotangent, ocean, depth):
    tiles, levs = lax.axis_size("tile"), lax.axis_size("lev")
    plan = Plan(state.shape, tiles, levs)
    height, width, model = plan.height, plan.width, plan.model
    sides = 1 if plan.compact else 2

    def bind(body, *first):
        return lambda *refs: body(*first, *refs)

    def swap(block, axis, first):
        return lax.ppermute(block, axis, swap_pairs(lax.axis_size(axis), first))

    rows_e, rows_o, *near = pl.pallas_call(
        bind(stage_cut, plan),
        name="stage_cut",
        out_shape=[jax.ShapeDtypeStruct(plan.edge, BF16)] * 2
        + [jax.ShapeDtypeStruct(plan.own[1:] + (model,), BF16)] * sides,
        in_specs=[pl.BlockSpec(memory_space=pl.ANY)],
        out_specs=[VMEM] * (2 + sides),
        scratch_shapes=[pltpu.SemaphoreType.DMA((2 + sides,))],
        compiler_params=pltpu.CompilerParams(vmem_limit_bytes=2**20),
        cost_estimate=pl.CostEstimate(flops=20 * 10**9, bytes_accessed=2**20, transcendentals=0),
    )(state)
    near = [swap(edge, "lev", side) for side, edge in enumerate(near)]
    rows_e = swap(rows_e, "tile", 0)
    rows_o = swap(rows_o, "tile", 1)
    live = pltpu.SMEM(((plan.levels_n + 2) * plan.tall,), jnp.int32)
    own_cells = plan.own + (model,)
    qs, us, mid = call(
        bind(stage_own, plan),
        "stage_own",
        [(own_cells, BF16), (own_cells, BF16), ((plan.slots_n,) + plan.own[1:] + (2 * model,), BF16)],
        [ocean, depth, state, w_qkv, w_out, cotangent, *near],
        [live],
        cost=4 * 10**9,
    )
    rows_e, qs = lax.optimization_barrier((rows_e, qs))
    rows = model // (tiles * levs)
    if levs == 2 and rows % 8 == 0:
        share = (tiles, rows, 4 * model)
        sums = [(share, F32), (share, BF16)]
    else:
        sums = [((model, 4 * model), F32)]
    keys_n = 3 * (PAIR + 2 * REACH) * width
    masks_n = 2 if plan.compact else plan.blocks_n
    masks = pltpu.VMEM((masks_n, keys_n, plan.queries_n), F32)
    weights = (HEADS // GROUP,) + plan.wide + (plan.blocks_n * plan.queries_n,)
    carried = [
        (plan.wide + (model,), BF16),
        (plan.wide + (2 * model,), BF16),
        (weights, BF16),
        (weights, BF16),
        (own_cells, BF16),
        (own_cells, BF16),
    ]
    side = call(
        bind(stage_side, plan),
        "stage_side",
        carried[:2],
        [state, rows_e, mid, w_qkv],
        cost=2 * 10**9,
    )
    rows_o, *side = lax.optimization_barrier((rows_o, *side))
    lev_in = []
    for n in range(sides):
        lev_in += [near[n], swap(rows_e, "lev", n), swap(rows_o, "lev", n)]
    held = call(
        bind(stage_inner, plan),
        "stage_inner",
        carried,
        [ocean, depth, rows_o, qs, us, w_qkv, *side],
        [masks, live],
        mib=16,
        cost=8 * 10**9,
        aliases={6: 0, 7: 1},
    )
    ins = [ocean, depth, state, qs, us, mid, w_qkv, cotangent, *lev_in, *held]
    _, _, _, _, attn, dq, dkv16, *sums = call(
        bind(stage_attend, plan, len(sums)),
        "stage_attend",
        carried + [(plan.wide + (2 * model,), BF16)] + sums,
        ins,
        [masks, live],
        mib=20,
        cost=16 * 10**9,
        aliases={len(ins) - len(held) + i: i for i in range(len(held))},
    )
    edge_kind = (plan.wide[1:] + (model,), BF16)
    inner, part_e, part_o, *edges = call(
        bind(stage_out, plan),
        "stage_out",
        [(own_cells, F32), (plan.edge, F32), (plan.edge, F32)] + [edge_kind] * sides,
        [dkv16, w_qkv],
        [pltpu.VMEM(plan.wide[1:] + (model,), F32)],
        cost=4 * 10**9,
    )
    edges = [swap(edge, "lev", side) for side, edge in enumerate(edges)]
    send_e, send_o, out, own = call(
        bind(stage_fold, plan),
        "stage_fold",
        [(plan.edge, BF16)] * 2 + [(own_cells, BF16), (own_cells, F32)],
        [part_e, part_o, inner, state, cotangent, attn, dq, w_qkv, w_out, *edges],
        [pltpu.VMEM(plan.edge, F32)],
    )

    if len(sums) == 2:
        x, parts = sums[0], [lax.ppermute(sums[1], "lev", swap_pairs(levs, 0))]
    else:
        x, parts = reduce_levels(sums[0], tiles, levs), []
    stride = 1
    for radix in digits(tiles):
        share = (x.shape[0] // radix,) + x.shape[1:]
        x, *pieces = call(
            bind(stage_split, len(parts), radix, stride),
            "stage_split",
            [(share, F32)] + [(share, BF16)] * (radix - 1),
            [x, *parts],
        )
        sent = {}
        for k in range(len(pieces))[::-1]:
            sent[k] = lax.ppermute(pieces[k], "tile", xor_route(tiles, (k + 1) * stride))
        parts = [sent[k] for k in range(len(pieces))]
        if stride == 1:
            send_e, send_o, parts[2] = lax.optimization_barrier((send_e, send_o, parts[2]))
        stride *= radix
    back_e = swap(send_e, "tile", 0)
    back_o = swap(send_o, "tile", 1)
    (d_state,) = call(
        bind(stage_last, plan),
        "stage_last",
        [(own_cells, BF16)],
        [own, back_e, back_o, *edges],
        [pltpu.VMEM(own_cells, F32)],
    )
    d_state, parts[-1] = lax.optimization_barrier((d_state, parts[-1]))
    d_qkv, d_out = call(
        stage_sum,
        "stage_sum",
        [((rows, 3 * model), F32), ((rows, model), F32)],
        [x, *parts],
    )
    return (out, d_state, d_qkv, d_out)


def solution(mesh):
    placed = (P("lev", "tile", None, None), P(), P(), P("lev", "tile", None, None), P(), P())
    return jax.shard_map(
        local,
        mesh=mesh,
        in_specs=placed,
        out_specs=(
            P("lev", "tile", None, None),
            P("lev", "tile", None, None),
            P(("tile", "lev"), None),
            P(("tile", "lev"), None),
        ),
        check_vma=False,
    )
```

```python
import jax
import jax.numpy as jnp
from jax import lax
from jax.experimental import pallas as pl
from jax.experimental.pallas import tpu as pltpu
from jax.sharding import PartitionSpec as P

HEADS = 8
BROWS = 4
REACH = 3
GROUP = 4
PAIR = 2
LOW = -1e30
F32 = jnp.float32
BF16 = jnp.bfloat16
SMEM = pl.BlockSpec(memory_space=pltpu.SMEM)
VMEM = pl.BlockSpec(memory_space=pltpu.VMEM)


def dot(a, b, ca, cb):
    return lax.dot_general(a, b, (((ca,), (cb,)), ((), ())), preferred_element_type=F32)


def swap_pairs(count, first):
    route = []
    for i in range(first, count - 1, 2):
        route += [(i, i + 1), (i + 1, i)]
    return route


def call(body, name, outs, ins, scratch=(), mib=8, cost=10**6, aliases={}):
    return pl.pallas_call(
        body,
        name=name,
        out_shape=[jax.ShapeDtypeStruct(shape, kind) for shape, kind in outs],
        in_specs=[SMEM if x.dtype == jnp.int32 else VMEM for x in ins],
        out_specs=[VMEM] * len(outs),
        scratch_shapes=list(scratch),
        compiler_params=pltpu.CompilerParams(vmem_limit_bytes=mib * 2**20),
        input_output_aliases=aliases,
        cost_estimate=pl.CostEstimate(flops=cost, bytes_accessed=2**20, transcendentals=0),
    )(*ins)


class Plan:
    def __init__(self, shape, tiles, levs):
        self.levels_n, self.height, self.width, self.model = shape
        self.tiles, self.levs = tiles, levs
        self.tall = self.height + 2 * REACH
        self.compact = levs == 2 and self.levels_n == 2 and self.height == 2 * PAIR
        self.blocks_n = self.levels_n * self.height // PAIR
        self.lanes_n = GROUP * self.model // HEADS
        self.queries_n = GROUP * PAIR * self.width
        self.slots_n = self.levels_n + 2 - self.compact
        self.own = (self.levels_n, self.height, self.width)
        self.wide = (self.slots_n, self.tall, self.width)
        self.edge = (self.levels_n, REACH, self.width, self.model)

    def places(self):
        tile_odd = lax.rem(lax.axis_index("tile"), 2)
        lev_odd = lax.rem(lax.axis_index("lev"), 2)
        end = self.height + REACH
        self.even = tile_odd == 0
        self.at_e = jnp.where(tile_odd == 0, end, 0)
        self.at_o = jnp.where(tile_odd == 0, 0, end)
        self.off = 1 - lev_odd if self.compact else 0
        last = self.levels_n + 1
        self.slot_e = jnp.where(lev_odd == 0, last, 0) - self.off
        self.slot_o = jnp.where(lev_odd == 0, 0, last)
        self.first = 1 - self.off
        self.edge_e = jnp.where(lev_odd == 0, self.levels_n - 1, 0)
        self.edge_o = jnp.where(lev_odd == 0, 0, self.levels_n - 1)
        if self.compact:
            far = [(self.edge_o, r0, 2, self.first, 1) for r0 in (0, PAIR)]
            near = [(self.edge_e, r0, 3, 0, self.off) for r0 in (0, PAIR)]
            self.blocks = [far[0], near[0], near[1], far[1]]
        else:
            rows = range(0, self.height, PAIR)
            self.blocks = [(l, r0, 3, l, l) for l in range(self.levels_n) for r0 in rows]

    def liveness(self, ocean, depth, live):
        tile = lax.axis_index("tile")
        lev = lax.axis_index("lev")
        total_rows = self.height * self.tiles
        total_levels = self.levels_n * self.levs
        for r in range(self.tall):
            row = tile * self.height - REACH + r
            block_at = lax.div(jnp.clip(row, 0, total_rows - 1), BROWS)
            good = (row >= 0) & (row < total_rows) & (ocean[block_at] == 1)
            deep = depth[block_at]
            for l in range(self.levels_n + 2):
                at = lev * self.levels_n - 1 + l
                ok = good & (at >= 0) & (at < total_levels) & (at < deep)
                live[l * self.tall + r] = ok.astype(jnp.int32)

    def alive(self, live, level, row):
        return live[level * self.tall + row]


def stage_cut(plan, state, rows_e, rows_o, *refs):
    near, sems = refs[:-1], refs[-1]
    top = plan.height - REACH
    plan.places()
    at_e, at_o = jnp.where(plan.even, top, 0), jnp.where(plan.even, 0, top)
    cuts = [(state.at[:, pl.ds(at_e, REACH)], rows_e), (state.at[:, pl.ds(at_o, REACH)], rows_o)]
    cuts += [(state.at[level], edge) for level, edge in zip((plan.edge_e, plan.edge_o), near)]
    copies = [pltpu.make_async_copy(a, b, sems.at[i]) for i, (a, b) in enumerate(cuts)]
    for copy in copies:
        copy.start()
    for copy in copies:
        copy.wait()


def stage_own(plan, ocean, depth, state, w_qkv, w_out, cot, *refs):
    near, (qs, us, mid, live) = refs[:-4], refs[-4:]
    height, width, model = plan.own[1:] + (plan.model,)
    cells = height * width
    head = model // HEADS
    plan.places()
    plan.liveness(ocean, depth, live)

    def pairs(x):
        y = dot(x.reshape(cells, model), w_qkv[:, model:], 1, 0).astype(BF16)
        return y.reshape(height, width, 2 * model)

    for l in range(plan.levels_n):
        mid[plan.first + l] = pairs(state[l])
        flat = state[l].reshape(cells, model)
        q = dot(flat, w_qkv[:, :model], 1, 0).astype(BF16) * jnp.asarray(head**-0.5, BF16)
        qs[l] = q.reshape(height, width, model)
        u = dot(cot[l].reshape(cells, model), w_out[...], 1, 1).astype(BF16)
        u = u.reshape(height, width, model)
        for r in range(height):
            us[l, r] = u[r] * plan.alive(live, l + 1, REACH + r).astype(F32).astype(BF16)
    mid[plan.slot_e] = pairs(near[0][...])
    if not plan.compact:
        mid[plan.slot_o] = pairs(near[1][...])


def spread(plan, x):
    lane_head = lax.broadcasted_iota(jnp.int32, x.shape, 1) // (plan.model // HEADS)
    return jnp.concatenate(
        [jnp.where(lane_head == h, x, jnp.zeros_like(x)) for h in range(GROUP)], axis=0
    )


def group_lanes(plan, g):
    lanes = slice(g * plan.lanes_n, (g + 1) * plan.lanes_n)
    return lanes, slice(plan.model + lanes.start, plan.model + lanes.stop)


def spread_block(plan, x, block, lanes):
    l, r0 = block[:2]
    return spread(plan, x[l, r0 : r0 + PAIR, :, lanes].reshape(PAIR * plan.width, plan.lanes_n))


def attention(plan, numbers, live, qs, us, kv, bias, prob, grad, attn, dq):
    width, lanes_n, queries_n = plan.width, plan.lanes_n, plan.queries_n
    span = PAIR + 2 * REACH
    block_n = PAIR * width
    head = plan.model // HEADS
    lane_head = lax.broadcasted_iota(jnp.int32, (block_n, lanes_n), 1) // head
    query = lax.broadcasted_iota(jnp.int32, (width, queries_n), 1) % block_n
    query_row = query // width
    query_col = query % width
    key_col = lax.broadcasted_iota(jnp.int32, (width, queries_n), 0)
    near_col = jnp.abs(key_col - query_col) <= REACH

    def gather(x):
        total = jnp.where(lane_head == 0, x[:block_n], 0.0)
        for h in range(1, GROUP):
            total = jnp.where(lane_head == h, x[h * block_n : (h + 1) * block_n], total)
        return total

    def scores(slot, number, g):
        block = plan.blocks[number]
        l, r0, depth_n, base, _ = block
        keys_n = depth_n * span * width
        lanes, lanes_v = group_lanes(plan, g)
        q = spread_block(plan, qs, block, lanes)
        u = spread_block(plan, us, block, lanes)
        k = kv[pl.ds(base, depth_n), r0 : r0 + span, :, lanes].reshape(keys_n, lanes_n)
        v = kv[pl.ds(base, depth_n), r0 : r0 + span, :, lanes_v].reshape(keys_n, lanes_n)
        return k, v, dot(k, q, 1, 1) + bias[slot, :keys_n], dot(v, u, 1, 1)

    def weigh(s, dp):
        e = jnp.exp(s - jnp.max(s, axis=0, keepdims=True))
        inv = 1.0 / jnp.sum(e, axis=0, keepdims=True)
        delta = jnp.sum(e * dp, axis=0, keepdims=True) * inv
        p = e * inv
        return p.astype(BF16), (p * (dp - delta)).astype(BF16)

    def give(number, g, p16, ds16, k, v):
        l, r0, depth_n, base, _ = plan.blocks[number]
        lanes = group_lanes(plan, g)[0]
        at = slice(number * queries_n, (number + 1) * queries_n)
        tiled = (depth_n, span, width, queries_n)
        prob[g, pl.ds(base, depth_n), r0 : r0 + span, :, at] = p16.reshape(tiled)
        grad[g, pl.ds(base, depth_n), r0 : r0 + span, :, at] = ds16.reshape(tiled)
        a = gather(dot(p16, v, 0, 0))
        for r in range(PAIR):
            alive = plan.alive(live, l + 1, REACH + r0 + r).astype(F32)
            attn[l, r0 + r, :, lanes] = (a[r * width : (r + 1) * width] * alive).astype(BF16)
        b = gather(dot(ds16, k, 0, 0)) * (head**-0.5)
        dq[l, r0 : r0 + PAIR, :, lanes] = b.astype(BF16).reshape(PAIR, width, lanes_n)

    def mask(slot, number):
        _, r0, depth_n, _, base_level = plan.blocks[number]
        for dl in range(depth_n):
            for kr in range(span):
                alive = plan.alive(live, base_level + dl, r0 + kr) == 1
                near = near_col & (jnp.abs(query_row + REACH - kr) <= REACH)
                at = (dl * span + kr) * width
                bias[slot, at : at + width] = jnp.where(near & alive, 0.0, LOW)

    jobs = []
    for i, number in enumerate(numbers):
        mask(i, number)
        jobs += [(i, number, g) for g in range(HEADS // GROUP)]
    ready = [scores(*jobs[0])]
    for i, job in enumerate(jobs):
        if i + 1 < len(jobs):
            ready.append(scores(*jobs[i + 1]))
        k, v, s, dp = ready[i]
        give(*job[1:], *weigh(s, dp), k, v)


def sum_keys(plan, qs, us, prob, grad, dkv16):
    n = plan.queries_n
    if plan.compact:
        own, edge = pl.ds(plan.first, plan.levels_n), pl.ds(plan.slot_e, 1)
        end = plan.tall
        parts = [(own, plan.levels_n, 0, PAIR, 0, 2), (own, plan.levels_n, PAIR, end - PAIR, 0, 4)]
        parts += [(own, plan.levels_n, end - PAIR, end, 2, 4), (edge, 1, 0, PAIR, 1, 2)]
        parts += [(edge, 1, PAIR, end - PAIR, 1, 3), (edge, 1, end - PAIR, end, 2, 3)]
    else:
        parts = [(pl.ds(i, 1), 1, 0, plan.tall, 0, plan.blocks_n) for i in range(plan.slots_n)]
    for g in range(HEADS // GROUP):
        lanes, lanes_v = group_lanes(plan, g)
        for source, weights, at in ((qs, grad, lanes), (us, prob, lanes_v)):
            x = [spread_block(plan, source, block, lanes) for block in plan.blocks]
            x = jnp.concatenate(x, axis=0)
            for slots, slots_n, low, high, k0, k1 in parts:
                w = weights[g, slots, low:high, :, k0 * n : k1 * n]
                w = w.reshape(slots_n * (high - low) * plan.width, (k1 - k0) * n)
                y = dot(w, x[k0 * n : k1 * n], 1, 0).astype(BF16)
                dkv16[slots, low:high, :, at] = y.reshape(slots_n, high - low, plan.width, plan.lanes_n)


def project(plan, slot, ext, mid, w_qkv, kv):
    height, width = plan.own[1:]
    model = plan.model
    edge = REACH * width
    cells = [ext[slot, :REACH].reshape(edge, model), ext[slot, height + REACH :].reshape(edge, model)]
    pairs = dot(jnp.concatenate(cells, axis=0), w_qkv[:, model:], 1, 0).astype(BF16)
    kv[slot, :REACH] = pairs[:edge].reshape(REACH, width, 2 * model)
    kv[slot, height + REACH :] = pairs[edge:].reshape(REACH, width, 2 * model)
    kv[slot, REACH : height + REACH] = mid[slot]


def place_rows(plan, rows, at, w_qkv, ext, kv):
    slots = pl.ds(plan.first, plan.levels_n)
    ext[slots, pl.ds(at, REACH)] = rows[...]
    flat = rows[...].reshape(plan.levels_n * REACH * plan.width, plan.model)
    pairs = dot(flat, w_qkv[:, plan.model :], 1, 0).astype(BF16)
    kv[slots, pl.ds(at, REACH)] = pairs.reshape(plan.levels_n, REACH, plan.width, 2 * plan.model)


def stage_side(plan, state, rows_e, mid, w_qkv, ext, kv):
    plan.places()
    slots = pl.ds(plan.first, plan.levels_n)
    ext[slots, REACH : plan.height + REACH] = state[...]
    kv[slots, REACH : plan.height + REACH] = mid[slots]
    place_rows(plan, rows_e, plan.at_e, w_qkv, ext, kv)


def stage_inner(plan, ocean, depth, rows_o, qs, us, w_qkv, *refs):
    ext, kv, prob, grad, attn, dq, bias, live = refs[2:]
    plan.places()
    plan.liveness(ocean, depth, live)
    place_rows(plan, rows_o, plan.at_o, w_qkv, ext, kv)
    if plan.compact:
        attention(plan, (0, 3), live, qs, us, kv, bias, prob, grad, attn, dq)


def stage_attend(plan, sums_n, ocean, depth, state, qs, us, mid, w_qkv, cot, *refs):
    sides = 1 if plan.compact else 2
    lev_in, refs = refs[: 3 * sides], refs[3 * sides + 6 :]
    ext, kv, prob, grad, attn, dq, dkv16 = refs[:7]
    sums, (bias, live) = refs[7 : 7 + sums_n], refs[7 + sums_n :]
    levels_n, height, width = plan.own
    model, tall = plan.model, plan.tall
    plan.places()
    plan.liveness(ocean, depth, live)
    for side, (slot, level) in enumerate(((plan.slot_e, plan.edge_o), (plan.slot_o, plan.edge_e))):
        if side < sides:
            near, far_e, far_o = lev_in[3 * side : 3 * side + 3]
            ext[slot, REACH : height + REACH] = near[...]
            ext[slot, pl.ds(plan.at_e, REACH)] = far_e[level]
            ext[slot, pl.ds(plan.at_o, REACH)] = far_o[level]
            project(plan, slot, ext, mid, w_qkv, kv)
    if plan.compact:
        numbers = (1, 2)
    else:
        numbers = range(plan.blocks_n)
        prob[...] = jnp.zeros(prob.shape, BF16)
        grad[...] = jnp.zeros(grad.shape, BF16)
    attention(plan, numbers, live, qs, us, kv, bias, prob, grad, attn, dq)
    sum_keys(plan, qs, us, prob, grad, dkv16)
    cells = levels_n * height * width
    wide = plan.slots_n * tall * width

    def emit(at, x):
        n = x.shape[1]
        if sums_n == 1:
            sums[0][:, at : at + n] = x
            return
        keep, send = sums
        rows = model // (plan.tiles * plan.levs)
        x = x.reshape(plan.tiles, plan.levs, rows, n)
        mine = lax.axis_index("lev") == 0
        keep[:, :, at : at + n] = jnp.where(mine, x[:, 0], x[:, 1])
        send[:, :, at : at + n] = jnp.where(mine, x[:, 1], x[:, 0]).astype(BF16)

    emit(0, dot(state[...].reshape(cells, model), dq[...].reshape(cells, model), 0, 0))
    emit(3 * model, dot(attn[...].reshape(cells, model), cot[...].reshape(cells, model), 0, 0))
    for j in range(2):
        part = dkv16[:, :, :, j * model : (j + 1) * model].reshape(wide, model)
        emit((j + 1) * model, dot(ext[...].reshape(wide, model), part, 0, 0))


def stage_out(plan, dkv16, w_qkv, inner, rows_e, rows_o, *refs):
    edges, tmp = refs[:-1], refs[-1]
    levels_n, height, width = plan.own
    model, tall = plan.model, plan.tall
    plan.places()

    def back(slot):
        x = dot(dkv16[slot].reshape(tall * width, 2 * model), w_qkv[:, model:], 1, 1)
        return x.reshape(tall, width, model)

    for edge, slot in zip(edges, (plan.slot_e, plan.slot_o)):
        edge[...] = back(slot).astype(BF16)
    for l in range(levels_n):
        tmp[...] = back(plan.first + l)
        rows_e[l] = tmp[pl.ds(plan.at_e, REACH)]
        rows_o[l] = tmp[pl.ds(plan.at_o, REACH)]
        inner[l] = tmp[REACH : REACH + height]


def stage_fold(plan, rows_e, rows_o, inner, state, cot, attn, dq, w_qkv, w_out, *refs):
    edges, (send_e, send_o, out, own, acc) = refs[:-5], refs[-5:]
    levels_n, height, width = plan.own
    model = plan.model
    cells = height * width
    plan.places()
    for rows, at, send in ((rows_e, plan.at_e, send_e), (rows_o, plan.at_o, send_o)):
        acc[...] = rows[...]
        for edge, level in zip(edges, (plan.edge_e, plan.edge_o)):
            acc[level] += edge[pl.ds(at, REACH)].astype(F32)
        send[...] = acc[...].astype(BF16)
    for l in range(levels_n):
        x = cot[l].reshape(cells, model).astype(F32)
        x = x + dot(dq[l].reshape(cells, model), w_qkv[:, :model], 1, 1)
        own[l] = x.reshape(height, width, model) + inner[l]
        x = state[l].reshape(cells, model).astype(F32)
        x = x + dot(attn[l].reshape(cells, model), w_out[...], 1, 0)
        out[l] = x.astype(BF16).reshape(height, width, model)


def stage_last(plan, parts_n, own, back_e, back_o, x, *refs):
    parts, edges, (d_state, d_qkv, d_out, acc) = refs[:parts_n], refs[parts_n:-4], refs[-4:]
    plan.places()
    height = plan.height
    acc[...] = own[...]
    for edge, level in zip(edges, (plan.edge_e, plan.edge_o)):
        acc[level] += edge[REACH : REACH + height].astype(F32)
    top = height - REACH
    acc[:, pl.ds(jnp.where(plan.even, top, 0), REACH)] += back_e[...].astype(F32)
    acc[:, pl.ds(jnp.where(plan.even, 0, top), REACH)] += back_o[...].astype(F32)
    d_state[...] = acc[...].astype(BF16)
    y = x[0]
    for part in parts:
        y = y + part[0].astype(F32)
    cut = d_qkv.shape[1]
    d_qkv[...] = y[:, :cut]
    d_out[...] = y[:, cut:]


def stage_split(parts_n, radix, stride, x, *refs):
    parts, (own, *pieces) = refs[:parts_n], refs[parts_n:]
    digit = lax.rem(lax.div(lax.axis_index("tile"), stride), radix)
    for h in range(x.shape[0] // radix):
        for k in range(radix):
            at = h * radix + jnp.bitwise_xor(digit, k)
            y = x[at]
            for part in parts:
                y = y + part[at].astype(F32)
            if k == 0:
                own[h] = y
            else:
                pieces[k - 1][h] = y.astype(BF16)


def digits(count):
    sizes = []
    while count > 1:
        radix = 4 if count % 4 == 0 else 2
        sizes.append(radix)
        count //= radix
    return sizes


def xor_route(count, step):
    return [(i, i ^ step) for i in range(count)]


def reduce_levels(x, tiles, levs):
    rows, cols = x.shape
    x = x.reshape([tiles] + digits(levs)[::-1] + [rows // (tiles * levs), cols])
    stride = 1
    for radix in digits(levs):
        dim = x.ndim - 3
        digit = lax.rem(lax.div(lax.axis_index("lev"), stride), radix)
        total = lax.dynamic_index_in_dim(x, digit, dim, keepdims=False)
        for k in range(1, radix):
            piece = lax.dynamic_index_in_dim(x, jnp.bitwise_xor(digit, k), dim, keepdims=False)
            piece = lax.ppermute(piece.astype(BF16), "lev", xor_route(levs, k * stride))
            total = total + piece.astype(F32)
        x = total
        stride *= radix
    return x


def local(state, w_qkv, w_out, cotangent, ocean, depth):
    tiles, levs = lax.axis_size("tile"), lax.axis_size("lev")
    plan = Plan(state.shape, tiles, levs)
    height, width, model = plan.height, plan.width, plan.model
    sides = 1 if plan.compact else 2

    def bind(body, *first):
        return lambda *refs: body(*first, *refs)

    def swap(block, axis, first):
        return lax.ppermute(block, axis, swap_pairs(lax.axis_size(axis), first))

    rows_e, rows_o, *near = pl.pallas_call(
        bind(stage_cut, plan),
        name="stage_cut",
        out_shape=[jax.ShapeDtypeStruct(plan.edge, BF16)] * 2
        + [jax.ShapeDtypeStruct(plan.own[1:] + (model,), BF16)] * sides,
        in_specs=[pl.BlockSpec(memory_space=pl.ANY)],
        out_specs=[VMEM] * (2 + sides),
        scratch_shapes=[pltpu.SemaphoreType.DMA((2 + sides,))],
        compiler_params=pltpu.CompilerParams(vmem_limit_bytes=2**20),
        cost_estimate=pl.CostEstimate(flops=20 * 10**9, bytes_accessed=2**20, transcendentals=0),
    )(state)
    near = [swap(edge, "lev", side) for side, edge in enumerate(near)]
    rows_e = swap(rows_e, "tile", 0)
    rows_o = swap(rows_o, "tile", 1)
    live = pltpu.SMEM(((plan.levels_n + 2) * plan.tall,), jnp.int32)
    own_cells = plan.own + (model,)
    qs, us, mid = call(
        bind(stage_own, plan),
        "stage_own",
        [(own_cells, BF16), (own_cells, BF16), ((plan.slots_n,) + plan.own[1:] + (2 * model,), BF16)],
        [ocean, depth, state, w_qkv, w_out, cotangent, *near],
        [live],
        cost=4 * 10**9,
    )
    rows_e, qs = lax.optimization_barrier((rows_e, qs))
    rows = model // (tiles * levs)
    if levs == 2 and rows % 8 == 0:
        share = (tiles, rows, 4 * model)
        sums = [(share, F32), (share, BF16)]
    else:
        sums = [((model, 4 * model), F32)]
    keys_n = 3 * (PAIR + 2 * REACH) * width
    masks_n = 2 if plan.compact else plan.blocks_n
    masks = pltpu.VMEM((masks_n, keys_n, plan.queries_n), F32)
    weights = (HEADS // GROUP,) + plan.wide + (plan.blocks_n * plan.queries_n,)
    carried = [
        (plan.wide + (model,), BF16),
        (plan.wide + (2 * model,), BF16),
        (weights, BF16),
        (weights, BF16),
        (own_cells, BF16),
        (own_cells, BF16),
    ]
    side = call(
        bind(stage_side, plan),
        "stage_side",
        carried[:2],
        [state, rows_e, mid, w_qkv],
        cost=2 * 10**9,
    )
    rows_o, *side = lax.optimization_barrier((rows_o, *side))
    lev_in = []
    for n in range(sides):
        lev_in += [near[n], swap(rows_e, "lev", n), swap(rows_o, "lev", n)]
    held = call(
        bind(stage_inner, plan),
        "stage_inner",
        carried,
        [ocean, depth, rows_o, qs, us, w_qkv, *side],
        [masks, live],
        mib=16,
        cost=8 * 10**9,
        aliases={6: 0, 7: 1},
    )
    ins = [ocean, depth, state, qs, us, mid, w_qkv, cotangent, *lev_in, *held]
    _, _, _, _, attn, dq, dkv16, *sums = call(
        bind(stage_attend, plan, len(sums)),
        "stage_attend",
        carried + [(plan.wide + (2 * model,), BF16)] + sums,
        ins,
        [masks, live],
        mib=20,
        cost=16 * 10**9,
        aliases={len(ins) - len(held) + i: i for i in range(len(held))},
    )
    edge_kind = (plan.wide[1:] + (model,), BF16)
    inner, part_e, part_o, *edges = call(
        bind(stage_out, plan),
        "stage_out",
        [(own_cells, F32), (plan.edge, F32), (plan.edge, F32)] + [edge_kind] * sides,
        [dkv16, w_qkv],
        [pltpu.VMEM(plan.wide[1:] + (model,), F32)],
        cost=4 * 10**9,
    )
    edges = [swap(edge, "lev", side) for side, edge in enumerate(edges)]
    send_e, send_o, out, own = call(
        bind(stage_fold, plan),
        "stage_fold",
        [(plan.edge, BF16)] * 2 + [(own_cells, BF16), (own_cells, F32)],
        [part_e, part_o, inner, state, cotangent, attn, dq, w_qkv, w_out, *edges],
        [pltpu.VMEM(plan.edge, F32)],
    )

    if len(sums) == 2:
        x, parts = sums[0], [lax.ppermute(sums[1], "lev", swap_pairs(levs, 0))]
    else:
        x, parts = reduce_levels(sums[0], tiles, levs), []
    stride = 1
    for radix in digits(tiles):
        share = (x.shape[0] // radix,) + x.shape[1:]
        x, *pieces = call(
            bind(stage_split, len(parts), radix, stride),
            "stage_split",
            [(share, F32)] + [(share, BF16)] * (radix - 1),
            [x, *parts],
        )
        sent = {}
        for k in range(len(pieces))[::-1]:
            sent[k] = lax.ppermute(pieces[k], "tile", xor_route(tiles, (k + 1) * stride))
        parts = [sent[k] for k in range(len(pieces))]
        if stride == 1:
            send_e, send_o, parts[2] = lax.optimization_barrier((send_e, send_o, parts[2]))
        stride *= radix
    back_e = swap(send_e, "tile", 0)
    back_o = swap(send_o, "tile", 1)
    d_state, d_qkv, d_out = call(
        bind(stage_last, plan, len(parts)),
        "stage_last",
        [(own_cells, BF16), ((rows, 3 * model), F32), ((rows, model), F32)],
        [own, back_e, back_o, x, *parts, *edges],
        [pltpu.VMEM(own_cells, F32)],
    )
    return (out, d_state, d_qkv, d_out)


def solution(mesh):
    placed = (P("lev", "tile", None, None), P(), P(), P("lev", "tile", None, None), P(), P())
    return jax.shard_map(
        local,
        mesh=mesh,
        in_specs=placed,
        out_specs=(
            P("lev", "tile", None, None),
            P("lev", "tile", None, None),
            P(("tile", "lev"), None),
            P(("tile", "lev"), None),
        ),
        check_vma=False,
    )
```
